256 devices in a mesh: lat: 32 (over x, y, core), depth: 8 (over z).
Axes of the slice: x: 4, y: 4, z: 8, core: 2. Of those that a mesh axis runs over, the one named last changes fastest.
Arguments:
- own_basis: bfloat16 [32, 1280, 64, 128], P(None, 'lat', 'depth'), may hold values from -1 to 1
- left_margin: bfloat16 [32, 512, 64, 128], P(None, 'lat', 'depth'), may hold values from -1 to 1
- right_margin: bfloat16 [32, 512, 64, 128], P(None, 'lat', 'depth'), may hold values from -1 to 1
- permeability: float32 [1280, 64, 128], P('lat', 'depth'), may hold values from 0 to 21, as said below
- cluster_mask: int32 [1280, 64], P('lat', 'depth'), may hold values 0 or 1
- intersection_width: int32 [32, 8, 2], P('lat', 'depth'), may hold values from 0 to 16, as said below
Outputs:
- lateral_rows: float32 [32, 8, 3, 32, 32], P('lat', 'depth')
- vertical_rows: float32 [32, 8, 2, 3, 32, 32], P('lat', 'depth')
The draws below stay inside these ranges and needn't reach their ends.
Inputs may be any that keep to these rules, and one draw needn't show every extreme that they name: `intersection_width`: A subdomain's reach in east cells into its left (last index 0) and right (last index 1) neighbour: a multiple of 8, 0 exactly where that neighbour lies outside the grid, 8 or more otherwise, and 16 for at least one subdomain. `permeability`: Positive.
All inputs are finite; a program needn't handle non-finite values. No bound on the sum of `cluster_mask` on one device may be relied on, other than what follows from the above.
Results may differ from the reference program's by a relative error of at most 0.00036.
Values may be sent and summed in bfloat16 or wider, within the bound.
A program may use at most 128 MiB of HBM per device.

```python
import math
import jax
import jax.numpy as jnp
from jax import lax

K = 32
CE = 40
CD = 8
CN = 128
MARGIN = 16
LAT_SUBS = 32
DEPTH_SUBS = 8
NE = 1280
ND = 64


def shared_parts(key, east_index, owner_index):
    key_waves = jax.random.fold_in(key, 0)
    key_phases = jax.random.fold_in(key, 1)
    key_rough = jax.random.fold_in(key, 2)
    key_normal = jax.random.fold_in(key, 3)
    key_shifts = jax.random.fold_in(key, 5)
    key_mix = jax.random.fold_in(key, 6)
    waves = jax.random.uniform(key_waves, (2, 3), jnp.float32, 0.0, 2.0 * math.pi / 48.0)
    phases = jax.random.uniform(key_phases, (2,), jnp.float32, 0.0, 2.0 * math.pi)
    rough = jax.random.uniform(key_rough, (NE, ND, CN), jnp.float32, 0.5, 1.5)
    rows_count = east_index.shape[0]
    east_cells = east_index[:, None, None]
    depth_index = jnp.arange(ND, dtype=jnp.int32)[None, :, None]
    north_index = jnp.arange(CN, dtype=jnp.int32)[None, None, :]
    east_float = east_cells.astype(jnp.float32)
    depth_float = depth_index.astype(jnp.float32)
    north_float = north_index.astype(jnp.float32)
    smooth = jnp.cos(waves[0, 0] * east_float + waves[0, 1] * depth_float + waves[0, 2] * north_float + phases[0])
    smooth = smooth + jnp.cos(waves[1, 0] * east_float + waves[1, 1] * depth_float + waves[1, 2] * north_float + phases[1])
    gain = rough[east_cells, depth_index, north_index]
    common = smooth * 0.5 ** 0.5 * gain
    panel_normal = 0.7 * jnp.clip(jax.random.normal(key_normal, (K, NE, CN), jnp.float32), -4.0, 4.0)
    panels = panel_normal
    shifts = jax.random.randint(key_shifts, (LAT_SUBS, DEPTH_SUBS), 1, K, dtype=jnp.int32)
    mixing = jax.random.uniform(key_mix, (LAT_SUBS, DEPTH_SUBS), jnp.float32, 0.3, 0.7)
    panel_rows = panels[:, east_index]
    panel_depth = jnp.broadcast_to(panel_rows[:, :, None, :], (K, rows_count, DEPTH_SUBS, CN))
    vector_index = jnp.arange(K, dtype=jnp.int32)[:, None, None, None]
    order = (vector_index + shifts[owner_index][None, :, :, None]) % K
    order = jnp.broadcast_to(order, (K, rows_count, DEPTH_SUBS, CN)).astype(jnp.int32)
    shifted = jnp.take_along_axis(panel_depth, order, axis=0)
    mixed = panel_depth + mixing[owner_index][None, :, :, None] * shifted
    gain_blocks = gain.reshape(rows_count, DEPTH_SUBS, CD, CN)
    rough_part = (mixed[:, :, :, None, :] * gain_blocks[None]).reshape(K, rows_count, ND, CN)
    return (common, rough_part)


def combine_parts(key, east_index, owner_index, noise):
    common, rough_part = shared_parts(key, east_index, owner_index)
    basis_scale = (6.1 * CE * CD * CN) ** (-0.5)
    return (basis_scale * (common[None] + rough_part + 0.5 * noise)).astype(jnp.bfloat16)


def margin_east(offset):
    rows_all = jnp.arange(LAT_SUBS * MARGIN, dtype=jnp.int32)
    east_index = rows_all // MARGIN * CE + offset + rows_all % MARGIN
    return jnp.clip(east_index, 0, NE - 1).astype(jnp.int32)


def draw_own_basis(key, part):
    noise_key = jax.random.fold_in(key, 11)
    east_index = jnp.arange(NE, dtype=jnp.int32)
    owner_index = (east_index // CE).astype(jnp.int32)
    noise = 0.7 * jnp.clip(jax.random.normal(noise_key, (K, NE, ND, CN), jnp.float32), -4.0, 4.0)
    return combine_parts(key, east_index, owner_index, noise)


def draw_left_margin(key, part):
    noise_key = jax.random.fold_in(key, 12)
    east_index = margin_east(-MARGIN)
    owner_index = (jnp.arange(LAT_SUBS * MARGIN, dtype=jnp.int32) // MARGIN).astype(jnp.int32)
    noise = 0.7 * jnp.clip(jax.random.normal(noise_key, (K, LAT_SUBS * MARGIN, ND, CN), jnp.float32), -4.0, 4.0)
    return combine_parts(key, east_index, owner_index, noise)


def draw_right_margin(key, part):
    noise_key = jax.random.fold_in(key, 13)
    east_index = margin_east(CE)
    owner_index = (jnp.arange(LAT_SUBS * MARGIN, dtype=jnp.int32) // MARGIN).astype(jnp.int32)
    noise = 0.7 * jnp.clip(jax.random.normal(noise_key, (K, LAT_SUBS * MARGIN, ND, CN), jnp.float32), -4.0, 4.0)
    return combine_parts(key, east_index, owner_index, noise)


def draw_permeability(key, part):
    key = jax.random.fold_in(key, 21)
    key_layers, key_cells = jax.random.split(key, 2)
    layers_log = jax.random.uniform(key_layers, (ND,), jnp.float32, math.log(0.1), math.log(10.0))
    noise = jax.random.uniform(key_cells, (NE, ND, CN), jnp.float32, -0.7, 0.7)
    return jnp.exp(layers_log[None, :, None] + noise).astype(jnp.float32)


def draw_intersection_width(key, part):
    key = jax.random.fold_in(key, 31)
    widths = 8 * jax.random.randint(key, (LAT_SUBS, DEPTH_SUBS, 2), 1, MARGIN // 8 + 1, dtype=jnp.int32)
    east_index = jnp.arange(LAT_SUBS, dtype=jnp.int32)[:, None, None]
    side_index = jnp.arange(2, dtype=jnp.int32)[None, None, :]
    widths = jnp.where((east_index == 0) & (side_index == 0), 0, widths)
    widths = jnp.where((east_index == LAT_SUBS - 1) & (side_index == 1), 0, widths)
    widths = widths.at[LAT_SUBS // 2, 0, 0].set(MARGIN)
    return widths.astype(jnp.int32)


def plant(entries, stream_key, low, high):
    dims = entries.shape
    spot = [jax.random.randint(jax.random.fold_in(stream_key, axis), (), 0, dims[axis]) for axis in range(len(dims))]
    entries = entries.at[tuple(spot)].set(low)
    longest = dims.index(max(dims))
    spot[longest] = (spot[longest] + 1) % dims[longest]
    return entries.at[tuple(spot)].set(high)


def setup_inputs(seed: int = 0) -> dict:
    keys = jax.random.split(jax.random.key(seed), 7)
    return {
        "own_basis": draw_own_basis(jax.random.fold_in(keys[6], 71), 0),
        "left_margin": draw_left_margin(jax.random.fold_in(keys[6], 71), 0),
        "right_margin": draw_right_margin(jax.random.fold_in(keys[6], 71), 0),
        "permeability": draw_permeability(jax.random.fold_in(keys[6], 71), 0),
        "cluster_mask": plant((jax.random.randint(keys[4], (NE, ND), 0, 2) < 1).astype(jnp.int32), jax.random.fold_in(keys[4], 1), 0, 1),
        "intersection_width": draw_intersection_width(jax.random.fold_in(keys[6], 71), 0),
    }


diagonal_weight = 6.1

def scaled(factor, values):
    return (factor.astype(jnp.float32) * values.astype(jnp.float32)).astype(jnp.bfloat16)

def pair_gram(left_part, right_part):
    return jnp.dot(left_part.reshape(left_part.shape[0], -1), right_part.reshape(right_part.shape[0], -1).T, preferred_element_type=jnp.float32)

def energy(field_planes):
    inner_cells = field_planes[:, 1:-1]
    energy_sum = diagonal_weight * pair_gram(inner_cells, inner_cells)
    energy_sum = energy_sum - pair_gram(inner_cells, field_planes[:, 2:]) - pair_gram(inner_cells, field_planes[:, :-2])
    north_pairs = pair_gram(inner_cells[:, :, :, :-1], inner_cells[:, :, :, 1:])
    depth_pairs = pair_gram(inner_cells[:, :, :-1], inner_cells[:, :, 1:])
    return energy_sum - north_pairs - north_pairs.T - depth_pairs - depth_pairs.T

def keep_margins(left_part, right_part, widths):
    plane_index = jnp.arange(left_part.shape[1], dtype=jnp.int32)[None, :, None, None]
    kept_left = jnp.where(plane_index >= left_part.shape[1] - widths[0], left_part, jnp.zeros_like(left_part))
    kept_right = jnp.where(plane_index < widths[1], right_part, jnp.zeros_like(right_part))
    return (kept_left, kept_right)

def build_fields(own_field, kept_left, kept_right, scaling, from_west, from_east):
    west_strip, west_edge, west_scaling = from_west
    east_strip, east_edge, east_scaling = from_east
    east_cells = own_field.shape[1]
    margin = kept_left.shape[1]
    own_west = scaled(west_scaling[None], kept_left[:, margin - 1:])
    own_east = scaled(east_scaling[None], kept_right[:, :1])
    left_field = scaled(scaling[None, :margin], west_strip)
    right_field = scaled(scaling[None, east_cells - margin:], east_strip)
    return (own_field, own_west, own_east, left_field, west_edge, right_field, east_edge)

def lateral_blocks(pieces):
    own_field, own_west, own_east, left_field, west_edge, right_field, east_edge = pieces
    basis_count = own_field.shape[0]
    east_cells = own_field.shape[1]
    margin = left_field.shape[1]
    blank_planes = jnp.zeros((basis_count, 2) + own_field.shape[2:], jnp.bfloat16)
    whole_block = energy(jnp.concatenate([own_west, own_field, own_east], 1))
    west_self = jnp.concatenate([own_west, own_field[:, :margin + 2]], 1)
    west_other = jnp.concatenate([west_edge, left_field, blank_planes], 1)
    west_block = energy(jnp.concatenate([west_self, west_other], 0))
    east_self = jnp.concatenate([own_field[:, east_cells - margin - 2:], own_east], 1)
    east_other = jnp.concatenate([blank_planes, right_field, east_edge], 1)
    east_block = energy(jnp.concatenate([east_self, east_other], 0))
    zero_block = jnp.zeros((basis_count, basis_count), jnp.float32)
    split_at = basis_count
    first_row = jnp.stack([whole_block, west_block[:split_at, split_at:], east_block[:split_at, split_at:]])
    second_row = jnp.stack([west_block[split_at:, :split_at], west_block[split_at:, split_at:], zero_block])
    third_row = jnp.stack([east_block[split_at:, :split_at], zero_block, east_block[split_at:, split_at:]])
    return jnp.stack([first_row, second_row, third_row])

def depth_plane(pieces, plane_at):
    own_field, own_west, own_east, left_field, west_edge, right_field, east_edge = pieces
    basis_count = own_field.shape[0]
    east_cells = own_field.shape[1]
    margin = left_field.shape[1]
    gap_zeros = jnp.zeros((basis_count, east_cells - margin, own_field.shape[3]), jnp.bfloat16)
    left_plane = jnp.concatenate([left_field[:, :, plane_at], gap_zeros], 1)
    right_plane = jnp.concatenate([gap_zeros, right_field[:, :, plane_at]], 1)
    return jnp.concatenate([own_field[:, :, plane_at], left_plane, right_plane], 0)

def to_blocks(matrix, basis_count):
    return matrix.reshape(3, basis_count, 3, basis_count).transpose(0, 2, 1, 3)

def assemble(own_rows, west_rows, east_rows):
    left_block = own_rows[..., 1, :, :] + west_rows[..., 0, :, :]
    middle_block = own_rows[..., 0, :, :] + west_rows[..., 2, :, :] + east_rows[..., 1, :, :]
    right_block = own_rows[..., 2, :, :] + east_rows[..., 0, :, :]
    return jnp.stack([left_block, middle_block, right_block], -3)

def load(arrays, east_index, depth_index):
    own_basis, left_margin, right_margin, scale_all, intersection_width = arrays
    inside = (east_index >= 0) & (east_index < LAT_SUBS) & (depth_index >= 0) & (depth_index < DEPTH_SUBS)
    east_clip = jnp.clip(east_index, 0, LAT_SUBS - 1).astype(jnp.int32)
    depth_clip = jnp.clip(depth_index, 0, DEPTH_SUBS - 1).astype(jnp.int32)
    zero_index = jnp.zeros((), jnp.int32)
    basis_block = lax.dynamic_slice(own_basis, (zero_index, east_clip * CE, depth_clip * CD, zero_index), (K, CE, CD, CN))
    left_part = lax.dynamic_slice(left_margin, (zero_index, east_clip * MARGIN, depth_clip * CD, zero_index), (K, MARGIN, CD, CN))
    right_part = lax.dynamic_slice(right_margin, (zero_index, east_clip * MARGIN, depth_clip * CD, zero_index), (K, MARGIN, CD, CN))
    scaling = lax.dynamic_slice(scale_all, (east_clip * CE, depth_clip * CD, zero_index), (CE, CD, CN))
    scaling = jnp.where(inside, scaling, jnp.zeros((CE, CD, CN), jnp.bfloat16))
    widths = lax.dynamic_slice(intersection_width, (east_clip, depth_clip, zero_index), (1, 1, 2))[0, 0]
    widths = jnp.where(inside, widths, jnp.zeros((2,), jnp.int32))
    kept_left, kept_right = keep_margins(left_part, right_part, widths)
    return (basis_block, kept_left, kept_right, scaling)

def fields(arrays, east_index, depth_index):
    basis_block, kept_left, kept_right, scaling = load(arrays, east_index, depth_index)
    basis_west, left_west, right_west, scaling_west = load(arrays, east_index - 1, depth_index)
    basis_east, left_east, right_east, scaling_east = load(arrays, east_index + 1, depth_index)
    from_west = (right_west, scaled(scaling_west[None, CE - 1:], basis_west[:, CE - 1:]), scaling_west[CE - 1:])
    from_east = (left_east, scaled(scaling_east[None, :1], basis_east[:, :1]), scaling_east[:1])
    own_field = scaled(scaling[None], basis_block)
    return build_fields(own_field, kept_left, kept_right, scaling, from_west, from_east)

def subdomain_blocks(arrays, flat_index):
    east_index = flat_index // DEPTH_SUBS
    depth_index = flat_index % DEPTH_SUBS
    pieces = fields(arrays, east_index, depth_index)
    below_pieces = fields(arrays, east_index, depth_index - 1)
    above_pieces = fields(arrays, east_index, depth_index + 1)
    down_pairs = -pair_gram(depth_plane(pieces, 0), depth_plane(below_pieces, CD - 1))
    up_pairs = -pair_gram(depth_plane(pieces, CD - 1), depth_plane(above_pieces, 0))
    return jnp.stack([lateral_blocks(pieces), to_blocks(down_pairs, K), to_blocks(up_pairs, K)])

def reference(own_basis, left_margin, right_margin, permeability, cluster_mask, intersection_width):
    scale_all = jnp.sqrt(permeability * (0.05 + 0.95 * cluster_mask.astype(jnp.float32))[:, :, None]).astype(jnp.bfloat16)
    arrays = (own_basis, left_margin, right_margin, scale_all, intersection_width)
    flat_all = jnp.arange(LAT_SUBS * DEPTH_SUBS, dtype=jnp.int32)
    blocks = lax.map(lambda flat_index: subdomain_blocks(arrays, flat_index), flat_all)
    blocks = blocks.reshape((LAT_SUBS, DEPTH_SUBS, 3, 3, 3, K, K))
    padded = jnp.pad(blocks, ((1, 1), (0, 0), (0, 0), (0, 0), (0, 0), (0, 0), (0, 0)))
    west_rows = padded[:-2, :, :, 2]
    east_rows = padded[2:, :, :, 1]
    row_blocks = assemble(blocks[:, :, :, 0], west_rows, east_rows)
    return (row_blocks[:, :, 0], row_blocks[:, :, 1:])
```

```python
import functools

import jax
import jax.numpy as jnp
from jax import lax
from jax.experimental import pallas as pl
from jax.experimental.pallas import tpu as pltpu
from jax.sharding import PartitionSpec as P

MESH = pl.DeviceIdType.MESH
f32 = jnp.float32
bf16 = jnp.bfloat16
diagonal_weight = 6.1

CHUNKS = 4

STRIP_R, STRIP_L, EDGE_R, OWN_UP, OWN_DOWN, MARGIN_UP, MARGIN_DOWN, PART_R, PART_L, PART_UP, PART_DOWN = range(11)
BULK_R = 11
BULK_L = BULK_R + CHUNKS
REMOTE = BULK_L + CHUNKS

PERM, MASK, WIDTH, LEFT, RIGHT, OWN = range(6)


def nt(left, right):
    return lax.dot_general(left, right, (((1,), (1,)), ((), ())), preferred_element_type=f32)


def nn(left, right):
    return jnp.dot(left, right, preferred_element_type=f32)


def split(value):
    high = value.astype(bf16)
    return high, (value - high.astype(f32)).astype(bf16)


def kernel(
    lat_n, depth_n,
    own_hbm, left_hbm, right_hbm, perm_hbm, mask_hbm, width_hbm,
    lateral_ref, vertical_ref,
    own_v, left_v, right_v, perm_v, mask_v, width_s,
    scale_v, strip_out, strip_in, factor_v,
    field_v, high_v, low_v, edge_in,
    margin_v, mhigh_v, mlow_v,
    land_v, other_v,
    planes_v, above_v, mplanes_v, mabove_v,
    acc_v, part_out, part_in,
    local_sem, send_sem, recv_sem,
):
    basis, cells, layers, north = own_hbm.shape
    margin = left_hbm.shape[1]
    rows = basis * layers
    lat, dep = lax.axis_index("lat"), lax.axis_index("depth")
    right = (lax.rem(lat + 1, lat_n), dep)
    left = (lax.rem(lat + lat_n - 1, lat_n), dep)
    up = (lat, lax.rem(dep + 1, depth_n))
    down = (lat, lax.rem(dep + depth_n - 1, depth_n))

    def remote(index, src, dst, device):
        return pltpu.make_async_remote_copy(
            src_ref=src, dst_ref=dst, send_sem=send_sem.at[index], recv_sem=recv_sem.at[index],
            device_id=device, device_id_type=MESH,
        )

    def columns(plane, count):
        return pl.ds(pl.multiple_of(plane * north, north), count * north)

    barrier = pltpu.get_barrier_semaphore()
    for device in (right, left, up, down):
        pl.semaphore_signal(barrier, inc=1, device_id=device, device_id_type=MESH)

    local = [
        pltpu.make_async_copy(perm_hbm, perm_v, local_sem.at[PERM]),
        pltpu.make_async_copy(mask_hbm, mask_v, local_sem.at[MASK]),
        pltpu.make_async_copy(width_hbm, width_s, local_sem.at[WIDTH]),
        pltpu.make_async_copy(left_hbm, left_v, local_sem.at[LEFT]),
        pltpu.make_async_copy(right_hbm, right_v, local_sem.at[RIGHT]),
        pltpu.make_async_copy(own_hbm, own_v, local_sem.at[OWN]),
    ]
    for index in (PERM, MASK, WIDTH, OWN, LEFT, RIGHT):
        local[index].start()
    for index in (PERM, MASK, WIDTH):
        local[index].wait()

    factor = 0.05 + 0.95 * mask_v[...].astype(f32)
    scaling = jnp.sqrt(perm_v[...] * factor[:, :, None]).astype(bf16)
    scale_v[...] = scaling.astype(f32)
    left_width, right_width = width_s[0, 0, 0], width_s[0, 0, 1]
    strip_out[0, 0:margin] = scaling[cells - margin :]
    strip_out[0, margin] = jnp.full((layers, north), right_width.astype(f32), f32).astype(bf16)
    strip_out[1, 0:margin] = scaling[:margin]
    strip_out[1, margin] = jnp.full((layers, north), left_width.astype(f32), f32).astype(bf16)

    pl.semaphore_wait(barrier, 4)
    strip_r = remote(STRIP_R, strip_out.at[0], strip_in.at[0], right)
    strip_l = remote(STRIP_L, strip_out.at[1], strip_in.at[1], left)
    strip_r.start()
    strip_l.start()
    size = margin // CHUNKS
    bulk_r, bulk_l = [], []
    for c in range(CHUNKS):
        part = pl.ds(c * size, size)
        bulk_r.append(remote(BULK_R + c, right_hbm.at[:, part], land_v.at[0, :, part], right))
        bulk_l.append(remote(BULK_L + c, left_hbm.at[:, part], land_v.at[1, :, part], left))
        bulk_r[c].start()
        bulk_l[c].start()

    pick_row = lax.broadcasted_iota(jnp.int32, (2 * basis, rows), 0)
    pick_col = lax.broadcasted_iota(jnp.int32, (2 * basis, rows), 1)
    wanted = jnp.where(pick_row < basis, pick_row * layers + layers - 1, (pick_row - basis) * layers)
    pick = (pick_col == wanted).astype(f32).astype(bf16)

    lane = lax.broadcasted_iota(jnp.int32, (rows, north), 1)
    layer = lax.rem(lax.broadcasted_iota(jnp.int32, (rows, north), 0), layers)
    zero_plane = jnp.zeros((rows, north), bf16)
    field_v[:, 0:north] = zero_plane
    field_v[:, (cells + 1) * north : (cells + 2) * north] = zero_plane

    def scaled(values, factors):
        return (values.astype(f32) * factors[None]).reshape(rows, north).astype(bf16)

    local[OWN].wait()
    group = 4

    def own_group(step, _):
        first = step * group
        for j in range(group):
            field_v[:, columns(first + 1 + j, 1)] = scaled(own_v[:, first + j], scale_v[first + j])
        planes_v[:, columns(first, group)] = nn(pick, field_v[:, columns(first + 1, group)]).astype(bf16)
        return _

    lax.fori_loop(0, cells // group, own_group, 0)
    own_up = remote(OWN_UP, planes_v.at[0:basis], above_v.at[basis : 2 * basis], up)
    own_down = remote(OWN_DOWN, planes_v.at[basis : 2 * basis], above_v.at[0:basis], down)
    own_up.start()
    own_down.start()
    edge_r = remote(EDGE_R, field_v.at[:, pl.ds(cells * north, north)], edge_in, right)
    edge_r.start()

    strip_r.wait_recv()
    strip_l.wait_recv()
    at = lax.broadcasted_iota(jnp.int32, (margin, layers, north), 0).astype(f32)
    zero_factor = jnp.zeros((margin, layers, north), f32)
    from_left = strip_in[0].astype(f32)
    from_right = strip_in[1].astype(f32)
    factor_v[0] = jnp.where(at >= margin - left_width.astype(f32), from_left[:margin], zero_factor)
    factor_v[1] = jnp.where(at < right_width.astype(f32), from_right[:margin], zero_factor)
    factor_v[2] = jnp.where(at < from_left[margin:], scale_v[0:margin], zero_factor)
    factor_v[3] = jnp.where(at >= margin - from_right[margin:], scale_v[cells - margin : cells], zero_factor)

    local[LEFT].wait()
    local[RIGHT].wait()
    for side, source in ((0, left_v), (1, right_v)):
        margin_v[side, :, margin * north : (margin + 1) * north] = zero_plane

        def margin_group(step, _, side=side, source=source):
            first = step * group
            for j in range(group):
                margin_v[side, :, columns(first + j, 1)] = scaled(source[:, first + j], factor_v[side, first + j])
            mplanes_v[side, :, columns(first, group)] = nn(
                pick, margin_v[side, :, columns(first, group)]
            ).astype(bf16)
            return _

        lax.fori_loop(0, margin // group, margin_group, 0)
    margin_up = remote(MARGIN_UP, mplanes_v.at[0, 0:basis], mabove_v.at[0], up)
    margin_down = remote(MARGIN_DOWN, mplanes_v.at[1, basis : 2 * basis], mabove_v.at[1], down)
    margin_up.start()
    margin_down.start()

    zero = jnp.zeros((rows, north), f32)

    def sublane_roll(value, shift):
        return pltpu.roll(value.reshape(basis, layers, north), shift, 1).reshape(rows, north)

    def own_operator(plane, _):
        here = field_v[:, columns(plane + 1, 1)].astype(f32)
        east = field_v[:, columns(plane, 1)].astype(f32) + field_v[:, columns(plane + 2, 1)].astype(f32)
        sides = jnp.where(lane > 0, pltpu.roll(here, 1, 1), zero) + jnp.where(
            lane < north - 1, pltpu.roll(here, north - 1, 1), zero
        )
        ends = jnp.where(layer > 0, sublane_roll(here, 1), zero) + jnp.where(
            layer < layers - 1, sublane_roll(here, layers - 1), zero
        )
        high, low = split(diagonal_weight * here - east - sides - ends)
        high_v[:, columns(plane, 1)] = high
        low_v[:, columns(plane, 1)] = low
        return _

    lax.fori_loop(0, cells, own_operator, 0)

    for side in range(2):

        def margin_operator(plane, _, side=side):
            here = margin_v[side, :, columns(plane, 1)].astype(f32)
            east = margin_v[side, :, columns(plane + 1, 1)].astype(f32)
            sides = jnp.where(lane < north - 1, pltpu.roll(here, north - 1, 1), zero)
            ends = jnp.where(layer < layers - 1, sublane_roll(here, layers - 1), zero)
            high, low = split(diagonal_weight * here - 2.0 * (east + sides + ends))
            mhigh_v[side, :, columns(plane, 1)] = high
            mlow_v[side, :, columns(plane, 1)] = low
            return _

        lax.fori_loop(0, margin, margin_operator, 0)

    first_edge = jnp.concatenate([field_v[:, north : 2 * north], field_v[:, cells * north : (cells + 1) * north]], 1)
    last_edge = jnp.concatenate(
        [margin_v[0, :, (margin - 1) * north : margin * north], margin_v[1, :, 0:north]], 1
    )
    acc_v[0] = nt(first_edge, -2.0 * last_edge)
    run = 8

    def own_gram(step, _):
        fields = field_v[:, columns(step * run + 1, run)]
        acc_v[0] += nt(fields, high_v[:, columns(step * run, run)]) + nt(fields, low_v[:, columns(step * run, run)])
        return _

    lax.fori_loop(0, cells // run, own_gram, 0)
    for side in range(2):

        def margin_gram(step, _, side=side):
            fields = margin_v[side, :, columns(step * run, run)]
            acc_v[0] += nt(fields, mhigh_v[side, :, columns(step * run, run)]) + nt(
                fields, mlow_v[side, :, columns(step * run, run)]
            )
            return _

        lax.fori_loop(0, margin // run, margin_gram, 0)

    same_layer = (
        lax.rem(lax.broadcasted_iota(jnp.int32, (rows, rows), 0), layers)
        == lax.rem(lax.broadcasted_iota(jnp.int32, (rows, rows), 1), layers)
    )
    gather = (
        lax.broadcasted_iota(jnp.int32, (rows, basis), 0) // layers
        == lax.broadcasted_iota(jnp.int32, (rows, basis), 1)
    ).astype(f32)

    def collapse(matrix):
        kept = jnp.where(same_layer, matrix, jnp.zeros_like(matrix))
        summed = jnp.sum(kept.reshape(basis, layers, rows), axis=1)
        return jnp.dot(summed, gather, precision=lax.Precision.HIGHEST, preferred_element_type=f32)

    own_block = collapse(acc_v[0])
    own_block = 0.5 * (own_block + own_block.T)

    own_up.wait_recv()
    own_down.wait_recv()
    across = nt(planes_v[...], above_v[...])
    margin_up.wait_recv()
    margin_down.wait_recv()
    left_bottom = mplanes_v[0, basis : 2 * basis]
    right_top = mplanes_v[1, 0:basis]
    across_down = across[basis:, basis:] + nt(left_bottom, mabove_v[0])
    across_up = across[:basis, :basis] + nt(right_top, mabove_v[1])
    margin_to_down = nt(mabove_v[0], left_bottom)
    margin_to_up = nt(mabove_v[1], right_top)

    edge_r.wait_recv()
    far_edge = edge_in[...]
    starts = (0, cells - margin)
    totals = [None, None]
    pairs = [None, None]
    pairs_t = [None, None]
    for c in range(CHUNKS):
        for side, bulk in ((0, bulk_r), (1, bulk_l)):
            bulk[c].wait_recv()
            for j in range(size):
                plane = c * size + j
                other_v[side, :, plane * north : (plane + 1) * north] = scaled(
                    land_v[side, :, plane], factor_v[2 + side, plane]
                )
            other = other_v[side, :, c * size * north : (c + 1) * size * north]
            span = pl.ds((starts[side] + c * size) * north, size * north)
            term = nt(other, high_v[:, span]) + nt(other, low_v[:, span])
            if side == 0 and c == 0:
                far = jnp.concatenate([far_edge, other[:, :north]], 1)
                near = jnp.concatenate(
                    [field_v[:, north : 2 * north], margin_v[0, :, (margin - 1) * north : margin * north]], 1
                )
                term = term + nt(far, -near)
            if c == 0:
                acc_v[1 + side] = term
            else:
                acc_v[1 + side] += term
            other_planes = nn(pick, other).astype(bf16)
            above = above_v[:, span]
            pair, pair_t = nt(above, other_planes), nt(other_planes, above)
            pairs[side] = pair if c == 0 else pairs[side] + pair
            pairs_t[side] = pair_t if c == 0 else pairs_t[side] + pair_t

    blank = jnp.zeros((basis, basis), f32)
    with_left, with_right = pairs
    part_out[2] = jnp.concatenate([with_left[:basis, :basis], margin_to_up, with_right[:basis, :basis], blank], 1)
    part_out[3] = jnp.concatenate([with_left[basis:, basis:], margin_to_down, with_right[basis:, basis:], blank], 1)
    part_up = remote(PART_UP, part_out.at[2], part_in.at[2], up)
    part_down = remote(PART_DOWN, part_out.at[3], part_in.at[3], down)
    part_up.start()
    part_down.start()

    fold = lax.broadcasted_iota(jnp.int32, (basis, 2 * basis), 1) < basis
    rows_of_left = collapse(acc_v[1])
    part_out[1] = jnp.concatenate(
        [jnp.where(fold, pairs_t[0][:basis], pairs_t[0][basis:]), rows_of_left, blank], 1
    )
    part_l = remote(PART_L, part_out.at[1], part_in.at[1], left)
    part_l.start()
    rows_of_right = collapse(acc_v[2])
    part_out[0] = jnp.concatenate(
        [jnp.where(fold, pairs_t[1][:basis], pairs_t[1][basis:]), rows_of_right, blank], 1
    )
    part_r = remote(PART_R, part_out.at[0], part_in.at[0], right)
    part_r.start()

    part_up.wait_recv()
    part_down.wait_recv()
    part_l.wait_recv()
    part_r.wait_recv()
    west, east, below, above = part_in[0], part_in[1], part_in[2], part_in[3]

    def inside(condition, block):
        return jnp.where(jnp.full(block.shape, condition.astype(jnp.int32), jnp.int32) > 0, block, jnp.zeros_like(block))

    has_west, has_east, has_below, has_above = lat > 0, lat < lat_n - 1, dep > 0, dep < depth_n - 1
    lateral_ref[0, 0, 0] = inside(has_west, rows_of_left.T + west[:, 2 * basis : 3 * basis])
    lateral_ref[0, 0, 1] = own_block
    lateral_ref[0, 0, 2] = inside(has_east, rows_of_right.T + east[:, 2 * basis : 3 * basis])
    vertical_ref[0, 0, 0, 0] = inside(has_below & has_west, -(below[:, :basis] + west[:, basis : 2 * basis]))
    vertical_ref[0, 0, 0, 1] = inside(has_below, -(below[:, basis : 2 * basis] + across_down))
    vertical_ref[0, 0, 0, 2] = inside(
        has_below & has_east, -(below[:, 2 * basis : 3 * basis] + east[:, basis : 2 * basis])
    )
    vertical_ref[0, 0, 1, 0] = inside(has_above & has_west, -(above[:, :basis] + west[:, :basis]))
    vertical_ref[0, 0, 1, 1] = inside(has_above, -(above[:, basis : 2 * basis] + across_up))
    vertical_ref[0, 0, 1, 2] = inside(has_above & has_east, -(above[:, 2 * basis : 3 * basis] + east[:, :basis]))

    for copy in [
        strip_r, strip_l, edge_r, own_up, own_down, margin_up, margin_down, part_up, part_down, part_l, part_r,
        *bulk_r, *bulk_l,
    ]:
        copy.wait_send()


def body(lat_n, depth_n, own_basis, left_margin, right_margin, permeability, cluster_mask, intersection_width):
    basis, cells, layers, north = own_basis.shape
    margin = left_margin.shape[1]
    rows = basis * layers
    any_space = pl.BlockSpec(memory_space=pl.ANY)
    vmem = pl.BlockSpec(memory_space=pltpu.VMEM)
    scratch = [
        pltpu.VMEM(own_basis.shape, bf16),
        pltpu.VMEM(left_margin.shape, bf16),
        pltpu.VMEM(right_margin.shape, bf16),
        pltpu.VMEM(permeability.shape, f32),
        pltpu.VMEM(cluster_mask.shape, jnp.int32),
        pltpu.SMEM(intersection_width.shape, jnp.int32),
        pltpu.VMEM((cells, layers, north), f32),
        pltpu.VMEM((2, margin + 1, layers, north), bf16),
        pltpu.VMEM((2, margin + 1, layers, north), bf16),
        pltpu.VMEM((4, margin, layers, north), f32),
        pltpu.VMEM((rows, (cells + 2) * north), bf16),
        pltpu.VMEM((rows, cells * north), bf16),
        pltpu.VMEM((rows, cells * north), bf16),
        pltpu.VMEM((rows, north), bf16),
        pltpu.VMEM((2, rows, (margin + 1) * north), bf16),
        pltpu.VMEM((2, rows, margin * north), bf16),
        pltpu.VMEM((2, rows, margin * north), bf16),
        pltpu.VMEM((2, basis, margin, layers, north), bf16),
        pltpu.VMEM((2, rows, margin * north), bf16),
        pltpu.VMEM((2 * basis, cells * north), bf16),
        pltpu.VMEM((2 * basis, cells * north), bf16),
        pltpu.VMEM((2, 2 * basis, margin * north), bf16),
        pltpu.VMEM((2, basis, margin * north), bf16),
        pltpu.VMEM((3, rows, rows), f32),
        pltpu.VMEM((4, basis, 4 * basis), f32),
        pltpu.VMEM((4, basis, 4 * basis), f32),
        pltpu.SemaphoreType.DMA((6,)),
        pltpu.SemaphoreType.DMA((REMOTE,)),
        pltpu.SemaphoreType.DMA((REMOTE,)),
    ]
    return pl.pallas_call(
        functools.partial(kernel, lat_n, depth_n),
        out_shape=(
            jax.ShapeDtypeStruct((1, 1, 3, basis, basis), f32),
            jax.ShapeDtypeStruct((1, 1, 2, 3, basis, basis), f32),
        ),
        in_specs=[any_space] * 6,
        out_specs=(vmem, vmem),
        scratch_shapes=scratch,
        compiler_params=pltpu.CompilerParams(
            collective_id=0, has_side_effects=True, vmem_limit_bytes=56 * 1024 * 1024
        ),
    )(own_basis, left_margin, right_margin, permeability, cluster_mask, intersection_width)


def solution(mesh):
    in_specs = (
        P(None, "lat", "depth", None),
        P(None, "lat", "depth", None),
        P(None, "lat", "depth", None),
        P("lat", "depth", None),
        P("lat", "depth"),
        P("lat", "depth", None),
    )
    out_specs = (P("lat", "depth", None, None, None), P("lat", "depth", None, None, None, None))
    return jax.shard_map(
        functools.partial(body, mesh.shape["lat"], mesh.shape["depth"]),
        mesh=mesh, in_specs=in_specs, out_specs=out_specs, check_vma=False,
    )
```

```python
import functools

import jax
import jax.numpy as jnp
from jax import lax
from jax.experimental import pallas as pl
from jax.experimental.pallas import tpu as pltpu
from jax.sharding import PartitionSpec as P

MESH = pl.DeviceIdType.MESH
f32 = jnp.float32
bf16 = jnp.bfloat16
diagonal_weight = 6.1

CHUNKS = (4, 4, 4, 4)

STRIP_R, STRIP_L, EDGE_R, OWN_UP, OWN_DOWN, MARGIN_UP, MARGIN_DOWN, PART_R, PART_L, PART_UP, PART_DOWN = range(11)
BULK_R = 11
BULK_L = BULK_R + len(CHUNKS)
REMOTE = BULK_L + len(CHUNKS)

PERM, MASK, WIDTH, LEFT, RIGHT, OWN = range(6)


def nt(left, right):
    return lax.dot_general(left, right, (((1,), (1,)), ((), ())), preferred_element_type=f32)


def nn(left, right):
    return jnp.dot(left, right, preferred_element_type=f32)


def split(value):
    high = value.astype(bf16)
    return high, (value - high.astype(f32)).astype(bf16)


def iota(shape, dim):
    return lax.broadcasted_iota(jnp.int32, shape, dim)


class Message:
    def __init__(self, copy, sends, receives):
        self.copy, self.sends, self.receives = copy, sends, receives

    def start(self):
        pl.when(self.sends)(self.copy.start)

    def wait_recv(self):
        pl.when(self.receives)(self.copy.wait_recv)

    def wait_send(self):
        pl.when(self.sends)(self.copy.wait_send)


def kernel(
    lat_n, depth_n,
    own_hbm, left_hbm, right_hbm, perm_hbm, mask_hbm, width_hbm,
    out_ref,
    own_v, left_v, right_v, perm_v, mask_v, width_s,
    scale_v, strip_out, strip_in, factor_v,
    field_v, high_v, low_v, north_v, edge_in,
    land_v, other_v,
    planes_v, mabove_v, stack_v,
    part_out, part_in,
    local_sem, send_sem, recv_sem,
):
    basis, cells, layers, north = own_hbm.shape
    margin = left_hbm.shape[1]
    rows = basis * layers
    lat, dep = lax.axis_index("lat"), lax.axis_index("depth")
    has_west, has_east, has_below, has_above = lat > 0, lat < lat_n - 1, dep > 0, dep < depth_n - 1
    right = (lax.rem(lat + 1, lat_n), dep)
    left = (lax.rem(lat + lat_n - 1, lat_n), dep)
    up = (lat, lax.rem(dep + 1, depth_n))
    down = (lat, lax.rem(dep + depth_n - 1, depth_n))
    ways = {
        "right": (right, has_east, has_west),
        "left": (left, has_west, has_east),
        "up": (up, has_above, has_below),
        "down": (down, has_below, has_above),
    }

    def remote(index, src, dst, way):
        device, sends, receives = ways[way]
        copy = pltpu.make_async_remote_copy(
            src_ref=src, dst_ref=dst, send_sem=send_sem.at[index], recv_sem=recv_sem.at[index],
            device_id=device, device_id_type=MESH,
        )
        return Message(copy, sends, receives)

    def columns(plane, count):
        return pl.ds(pl.multiple_of(plane * north, north), count * north)

    barrier = pltpu.get_barrier_semaphore()
    for device, exists, _ in ways.values():

        @pl.when(exists)
        def _(device=device):
            pl.semaphore_signal(barrier, inc=1, device_id=device, device_id_type=MESH)

    local = [
        pltpu.make_async_copy(perm_hbm, perm_v, local_sem.at[PERM]),
        pltpu.make_async_copy(mask_hbm, mask_v, local_sem.at[MASK]),
        pltpu.make_async_copy(width_hbm, width_s, local_sem.at[WIDTH]),
        pltpu.make_async_copy(left_hbm, left_v, local_sem.at[LEFT]),
        pltpu.make_async_copy(right_hbm, right_v, local_sem.at[RIGHT]),
        pltpu.make_async_copy(own_hbm, own_v, local_sem.at[OWN]),
    ]
    for index in (PERM, MASK, WIDTH, OWN, LEFT, RIGHT):
        local[index].start()
    for index in (PERM, MASK, WIDTH):
        local[index].wait()

    factor = 0.05 + 0.95 * mask_v[...].astype(f32)
    for cell in range(cells):
        wide = jnp.broadcast_to(factor[:, cell : cell + 1], (layers, north))
        scale_v[cell] = jnp.sqrt(perm_v[cell] * wide).astype(bf16).astype(f32)
    left_width, right_width = width_s[0, 0, 0], width_s[0, 0, 1]
    strip_out[0, 0:margin] = scale_v[cells - margin : cells].astype(bf16)
    strip_out[0, margin] = jnp.full((layers, north), right_width.astype(f32), f32).astype(bf16)
    strip_out[1, 0:margin] = scale_v[0:margin].astype(bf16)
    strip_out[1, margin] = jnp.full((layers, north), left_width.astype(f32), f32).astype(bf16)

    peers = (
        lax.div(lat + lat_n - 1, lat_n) + lax.div(2 * lat_n - 2 - lat, lat_n)
        + lax.div(dep + depth_n - 1, depth_n) + lax.div(2 * depth_n - 2 - dep, depth_n)
    )
    pl.semaphore_wait(barrier, peers)
    strip_r = remote(STRIP_R, strip_out.at[0], strip_in.at[0], "right")
    strip_l = remote(STRIP_L, strip_out.at[1], strip_in.at[1], "left")
    strip_r.start()
    strip_l.start()
    bulk_r, bulk_l, begins = [], [], []
    begin = 0
    for c, size in enumerate(CHUNKS):
        part = pl.ds(begin, size)
        bulk_r.append(remote(BULK_R + c, right_hbm.at[:, part], land_v.at[0, :, part], "right"))
        bulk_l.append(remote(BULK_L + c, left_hbm.at[:, part], land_v.at[1, :, part], "left"))
        bulk_r[c].start()
        bulk_l[c].start()
        begins.append(begin)
        begin += size

    pick_row = iota((2 * basis, rows), 0)
    wanted = jnp.where(pick_row < basis, pick_row * layers + layers - 1, (pick_row - basis) * layers)
    pick = (iota((2 * basis, rows), 1) == wanted).astype(f32).astype(bf16)

    first_own = margin + 1
    first_right = first_own + cells + 1
    for plane in (margin, first_right - 1, first_right + margin):
        field_v[:, plane * north : (plane + 1) * north] = jnp.zeros((rows, north), bf16)

    pair = 2 * north
    r, c = iota((pair, pair), 0), iota((pair, pair), 1)
    next_north = ((r - c == 1) & (r // north == c // north)).astype(f32).astype(bf16)
    in_pair = (((jnp.abs(r - c) == 1) & (r // north == c // north)) | (jnp.abs(r - c) == north)).astype(f32).astype(bf16)
    r, c = iota((rows, rows), 0), iota((rows, rows), 1)
    depth_sum = ((jnp.abs(r - c) == 1) & (r // layers == c // layers)).astype(f32).astype(bf16)

    def scaled(values, factors):
        return (values.astype(f32) * factors[None]).reshape(rows, north).astype(bf16)

    def fill(source, factors, first, count, group, side=None):
        def step(index, carry):
            base = index * group
            for j in range(group):
                field_v[:, columns(first + base + j, 1)] = scaled(source[:, base + j], factors(base + j))
            planes_v[:, columns(first + base, group)] = nn(
                pick, field_v[:, columns(first + base, group)]
            ).astype(bf16)
            if side is not None:
                for j in range(0, group, 2):
                    north_v[side, :, columns(base + j, 2)] = nn(
                        field_v[:, columns(first + base + j, 2)], next_north
                    ).astype(bf16)
            return carry

        lax.fori_loop(0, count // group, step, 0)

    local[OWN].wait()
    fill(own_v, lambda plane: scale_v[plane], first_own, cells, 8)
    own_columns = pl.ds(first_own * north, cells * north)
    own_up = remote(OWN_UP, planes_v.at[0:basis, own_columns], stack_v.at[basis : 2 * basis], "up")
    own_down = remote(OWN_DOWN, planes_v.at[basis : 2 * basis, own_columns], stack_v.at[0:basis], "down")
    own_up.start()
    own_down.start()
    edge_r = remote(EDGE_R, field_v.at[:, pl.ds((first_right - 2) * north, north)], edge_in, "right")
    edge_r.start()

    strip_r.wait_recv()
    strip_l.wait_recv()
    at = iota((margin, layers, north), 0).astype(f32)
    none = jnp.zeros((margin, layers, north), f32)
    from_left = strip_in[0].astype(f32)
    from_right = strip_in[1].astype(f32)
    factor_v[0] = jnp.where(at >= margin - left_width.astype(f32), from_left[:margin], none)
    factor_v[1] = jnp.where(at < right_width.astype(f32), from_right[:margin], none)
    factor_v[2] = jnp.where(at < from_left[margin:], scale_v[0:margin], none)
    factor_v[3] = jnp.where(at >= margin - from_right[margin:], scale_v[cells - margin : cells], none)
    local[LEFT].wait()
    local[RIGHT].wait()
    fill(left_v, lambda plane: factor_v[0, plane], 0, margin, 8, 0)
    fill(right_v, lambda plane: factor_v[1, plane], first_right, margin, 8, 1)
    margin_columns = (pl.ds(0, margin * north), pl.ds(first_right * north, margin * north))
    margin_up = remote(MARGIN_UP, planes_v.at[0:basis, margin_columns[0]], mabove_v.at[0], "up")
    margin_down = remote(
        MARGIN_DOWN, planes_v.at[basis : 2 * basis, margin_columns[1]], mabove_v.at[1], "down"
    )
    margin_up.start()
    margin_down.start()

    def operator(step, carry):
        for part in range(0, 8, 2):
            cell = step * 8 + part
            both = field_v[:, columns(first_own + cell, 2)]
            sums = nn(jnp.concatenate([both, depth_sum], 1), jnp.concatenate([in_pair, both], 0))
            for j, outer in ((0, -1), (1, 2)):
                middle = both[:, j * north : (j + 1) * north].astype(f32)
                beside = field_v[:, columns(first_own + cell + outer, 1)].astype(f32)
                value = diagonal_weight * middle - sums[:, j * north : (j + 1) * north] - beside
                high, low = split(value)
                high_v[:, columns(cell + j, 1)] = high
                low_v[:, columns(cell + j, 1)] = low
        return carry

    lax.fori_loop(0, cells // 8, operator, 0)

    r_layer, c_layer = lax.rem(r, layers), lax.rem(c, layers)
    same_layer = r_layer == c_layer
    half_weight = jnp.where(same_layer, 0.5 * diagonal_weight, jnp.where(c_layer - r_layer == 1, -1.0, 0.0))
    gather = (iota((rows, basis), 0) // layers == iota((rows, basis), 1)).astype(f32)

    def gathered(kept):
        summed = jnp.sum(kept.reshape(basis, layers, rows), axis=1)
        return jnp.dot(summed, gather, precision=lax.Precision.HIGHEST, preferred_element_type=f32)

    def collapse(matrix):
        return gathered(jnp.where(same_layer, matrix, jnp.zeros_like(matrix)))

    own_fields = field_v[:, first_own * north : (first_own + cells) * north]
    own_sum = nt(own_fields, high_v[...]) + nt(own_fields, low_v[...])
    squares, steps = [], []
    for side, first in ((0, 0), (1, first_right)):
        fields = field_v[:, first * north : (first + margin) * north]
        squares.append(nt(fields, fields))
        steps.append(nt(fields, field_v[:, (first + 1) * north : (first + margin + 1) * north]) + nt(fields, north_v[side]))

    def plane_of(plane):
        return field_v[:, plane * north : (plane + 1) * north]

    border = nt(
        jnp.concatenate([plane_of(margin - 1), plane_of(first_right - 2)], 1),
        jnp.concatenate([plane_of(first_own), plane_of(first_right)], 1),
    )
    own_block = gathered(
        half_weight * (squares[0] + squares[1])
        + jnp.where(same_layer, 0.5 * own_sum - (steps[0] + steps[1] + border), jnp.zeros_like(own_sum))
    )
    out_ref[1] = own_block + own_block.T

    own_up.wait_recv()
    own_down.wait_recv()
    across = nt(planes_v[:, first_own * north : (first_own + cells) * north], stack_v[0 : 2 * basis])
    margin_up.wait_recv()
    margin_down.wait_recv()
    left_bottom = planes_v[basis : 2 * basis, margin_columns[0]]
    right_top = planes_v[0:basis, margin_columns[1]]
    across_down = across[basis:, basis:] + nt(left_bottom, mabove_v[0])
    across_up = across[:basis, :basis] + nt(right_top, mabove_v[1])
    margin_to_down = nt(mabove_v[0], left_bottom)
    margin_to_up = nt(mabove_v[1], right_top)

    edge_r.wait_recv()
    starts = (0, cells - margin)
    totals = [None, None]
    for c, size in enumerate(CHUNKS):
        for side, bulk in ((0, bulk_r), (1, bulk_l)):
            bulk[c].wait_recv()
            for plane in range(begins[c], begins[c] + size):
                other_v[side, :, plane * north : (plane + 1) * north] = scaled(
                    land_v[side, :, plane], factor_v[2 + side, plane]
                )
            other = other_v[side, :, begins[c] * north : (begins[c] + size) * north]
            at_own = pl.ds((starts[side] + begins[c]) * north, size * north)
            term = nt(other, high_v[:, at_own]) + nt(other, low_v[:, at_own])
            if side == 0 and c == 0:
                far = jnp.concatenate([edge_in[...], other[:, :north]], 1)
                near = -jnp.concatenate([plane_of(first_own), plane_of(margin - 1)], 1)
                term = term + nt(far, near)
            totals[side] = term if c == 0 else totals[side] + term
            stack_v[2 * basis : 4 * basis, at_own] = nn(pick, other).astype(bf16)

    pairs = []
    for side in range(2):
        stack = stack_v[:, starts[side] * north : (starts[side] + margin) * north]
        pairs.append(nt(stack, stack))
    with_left, with_right = (both[: 2 * basis, 2 * basis :] for both in pairs)
    blank = jnp.zeros((basis, basis), f32)
    part_out[2] = jnp.concatenate([with_left[:basis, :basis], margin_to_up, with_right[:basis, :basis], blank], 1)
    part_out[3] = jnp.concatenate([with_left[basis:, basis:], margin_to_down, with_right[basis:, basis:], blank], 1)
    part_up = remote(PART_UP, part_out.at[2], part_in.at[2], "up")
    part_down = remote(PART_DOWN, part_out.at[3], part_in.at[3], "down")
    part_up.start()
    part_down.start()

    fold = iota((basis, 2 * basis), 1) < basis
    turned = [
        jnp.where(fold, both[2 * basis : 3 * basis, : 2 * basis], both[3 * basis :, : 2 * basis]) for both in pairs
    ]
    rows_of_left = collapse(totals[0])
    part_out[1] = jnp.concatenate([turned[0], rows_of_left, blank], 1)
    part_l = remote(PART_L, part_out.at[1], part_in.at[1], "left")
    part_l.start()
    rows_of_right = collapse(totals[1])
    part_out[0] = jnp.concatenate([turned[1], rows_of_right, blank], 1)
    part_r = remote(PART_R, part_out.at[0], part_in.at[0], "right")
    part_r.start()

    part_up.wait_recv()
    part_down.wait_recv()
    part_l.wait_recv()
    part_r.wait_recv()
    west, east, below, above = part_in[0], part_in[1], part_in[2], part_in[3]

    def inside(condition, block):
        return jnp.where(jnp.full(block.shape, condition.astype(jnp.int32), jnp.int32) > 0, block, jnp.zeros_like(block))

    out_ref[0] = inside(has_west, rows_of_left.T + west[:, 2 * basis : 3 * basis])
    out_ref[2] = inside(has_east, rows_of_right.T + east[:, 2 * basis : 3 * basis])
    out_ref[3] = inside(has_below & has_west, -(below[:, :basis] + west[:, basis : 2 * basis]))
    out_ref[4] = inside(has_below, -(below[:, basis : 2 * basis] + across_down))
    out_ref[5] = inside(has_below & has_east, -(below[:, 2 * basis : 3 * basis] + east[:, basis : 2 * basis]))
    out_ref[6] = inside(has_above & has_west, -(above[:, :basis] + west[:, :basis]))
    out_ref[7] = inside(has_above, -(above[:, basis : 2 * basis] + across_up))
    out_ref[8] = inside(has_above & has_east, -(above[:, 2 * basis : 3 * basis] + east[:, :basis]))

    for copy in [
        strip_r, strip_l, edge_r, own_up, own_down, margin_up, margin_down, part_up, part_down, part_l, part_r,
        *bulk_r, *bulk_l,
    ]:
        copy.wait_send()


def hand_out(blocks_ref, lateral_ref, vertical_ref, sems):
    copies = [
        pltpu.make_async_copy(blocks_ref.at[0:3], lateral_ref.at[0, 0], sems.at[0]),
        pltpu.make_async_copy(blocks_ref.at[3:6], vertical_ref.at[0, 0, 0], sems.at[1]),
        pltpu.make_async_copy(blocks_ref.at[6:9], vertical_ref.at[0, 0, 1], sems.at[2]),
    ]
    for copy in copies:
        copy.start()
    for copy in copies:
        copy.wait()


def body(lat_n, depth_n, own_basis, left_margin, right_margin, permeability, cluster_mask, intersection_width):
    basis, cells, layers, north = own_basis.shape
    margin = left_margin.shape[1]
    rows = basis * layers
    planes = cells + 2 * margin + 3
    any_space = pl.BlockSpec(memory_space=pl.ANY)
    vmem = pl.BlockSpec(memory_space=pltpu.VMEM)
    scratch = [
        pltpu.VMEM(own_basis.shape, bf16),
        pltpu.VMEM(left_margin.shape, bf16),
        pltpu.VMEM(right_margin.shape, bf16),
        pltpu.VMEM(permeability.shape, f32),
        pltpu.VMEM((layers, cells), jnp.int32),
        pltpu.SMEM(intersection_width.shape, jnp.int32),
        pltpu.VMEM((cells, layers, north), f32),
        pltpu.VMEM((2, margin + 1, layers, north), bf16),
        pltpu.VMEM((2, margin + 1, layers, north), bf16),
        pltpu.VMEM((4, margin, layers, north), f32),
        pltpu.VMEM((rows, planes * north), bf16),
        pltpu.VMEM((rows, cells * north), bf16),
        pltpu.VMEM((rows, cells * north), bf16),
        pltpu.VMEM((2, rows, margin * north), bf16),
        pltpu.VMEM((rows, north), bf16),
        pltpu.VMEM((2, basis, margin, layers, north), bf16),
        pltpu.VMEM((2, rows, margin * north), bf16),
        pltpu.VMEM((2 * basis, planes * north), bf16),
        pltpu.VMEM((2, basis, margin * north), bf16),
        pltpu.VMEM((4 * basis, cells * north), bf16),
        pltpu.VMEM((4, basis, 4 * basis), f32),
        pltpu.VMEM((4, basis, 4 * basis), f32),
        pltpu.SemaphoreType.DMA((6,)),
        pltpu.SemaphoreType.DMA((REMOTE,)),
        pltpu.SemaphoreType.DMA((REMOTE,)),
    ]
    blocks = pl.pallas_call(
        functools.partial(kernel, lat_n, depth_n),
        out_shape=jax.ShapeDtypeStruct((9, basis, basis), f32),
        in_specs=[any_space] * 6,
        out_specs=vmem,
        scratch_shapes=scratch,
        compiler_params=pltpu.CompilerParams(
            collective_id=0, has_side_effects=True, vmem_limit_bytes=56 * 1024 * 1024
        ),
    )(own_basis, left_margin, right_margin, permeability, cluster_mask.T, intersection_width)
    return pl.pallas_call(
        hand_out,
        out_shape=(
            jax.ShapeDtypeStruct((1, 1, 3, basis, basis), f32),
            jax.ShapeDtypeStruct((1, 1, 2, 3, basis, basis), f32),
        ),
        in_specs=[vmem],
        out_specs=(any_space, any_space),
        scratch_shapes=[pltpu.SemaphoreType.DMA((3,))],
    )(blocks)


def solution(mesh):
    in_specs = (
        P(None, "lat", "depth", None),
        P(None, "lat", "depth", None),
        P(None, "lat", "depth", None),
        P("lat", "depth", None),
        P("lat", "depth"),
        P("lat", "depth", None),
    )
    out_specs = (P("lat", "depth", None, None, None), P("lat", "depth", None, None, None, None))
    return jax.shard_map(
        functools.partial(body, mesh.shape["lat"], mesh.shape["depth"]),
        mesh=mesh, in_specs=in_specs, out_specs=out_specs, check_vma=False,
    )
```

```python
import functools

import jax
import jax.numpy as jnp
from jax import lax
from jax.experimental import pallas as pl
from jax.experimental.pallas import tpu as pltpu
from jax.sharding import PartitionSpec as P

MESH = pl.DeviceIdType.MESH
f32 = jnp.float32
bf16 = jnp.bfloat16
diagonal_weight = 6.1

CHUNKS = (8, 6, 2)

STRIP_R, STRIP_L, EDGE_R, MARGIN_UP, MARGIN_DOWN, PART_R, PART_L, PART_UP, PART_DOWN = range(9)
OWN_PARTS = (16, 24)
OWN_UP = 9
OWN_DOWN = OWN_UP + len(OWN_PARTS)
BULK_R = OWN_DOWN + len(OWN_PARTS)
BULK_L = BULK_R + len(CHUNKS)
REMOTE = BULK_L + len(CHUNKS)

PERM, MASK, WIDTH, LEFT, RIGHT, OWN = range(6)


def nt(left, right):
    return lax.dot_general(left, right, (((1,), (1,)), ((), ())), preferred_element_type=f32)


def nn(left, right):
    return jnp.dot(left, right, preferred_element_type=f32)


def split(value):
    high = value.astype(bf16)
    return high, (value - high.astype(f32)).astype(bf16)


def split_rest(value):
    high = value.astype(bf16)
    return high, value - high.astype(f32)


def iota(shape, dim):
    return lax.broadcasted_iota(jnp.int32, shape, dim)


class Message:
    def __init__(self, copy, sends, receives):
        self.copy, self.sends, self.receives = copy, sends, receives

    def start(self):
        pl.when(self.sends)(self.copy.start)

    def wait_recv(self):
        pl.when(self.receives)(self.copy.wait_recv)

    def wait_send(self):
        pl.when(self.sends)(self.copy.wait_send)


def kernel(
    lat_n, depth_n,
    own_hbm, left_hbm, right_hbm, perm_hbm, mask_hbm, width_hbm,
    out_ref,
    own_v, left_v, right_v, perm_v, mask_v, width_s,
    scale_v, strip_out, strip_in, factor_v,
    pick_v, shift_v, weight_v, gather_v,
    field_v, high_v, low_v, north_v, edge_in,
    land_v, other_v,
    planes_v, mabove_v, stack_v,
    part_out, part_in,
    local_sem, send_sem, recv_sem,
):
    basis, cells, layers, north = own_hbm.shape
    margin = left_hbm.shape[1]
    rows = basis * layers
    lat, dep = lax.axis_index("lat"), lax.axis_index("depth")
    has_west, has_east, has_below, has_above = lat > 0, lat < lat_n - 1, dep > 0, dep < depth_n - 1
    right = (lax.rem(lat + 1, lat_n), dep)
    left = (lax.rem(lat + lat_n - 1, lat_n), dep)
    up = (lat, lax.rem(dep + 1, depth_n))
    down = (lat, lax.rem(dep + depth_n - 1, depth_n))
    ways = {
        "right": (right, has_east, has_west),
        "left": (left, has_west, has_east),
        "up": (up, has_above, has_below),
        "down": (down, has_below, has_above),
    }

    def remote(index, src, dst, way):
        device, sends, receives = ways[way]
        copy = pltpu.make_async_remote_copy(
            src_ref=src, dst_ref=dst, send_sem=send_sem.at[index], recv_sem=recv_sem.at[index],
            device_id=device, device_id_type=MESH,
        )
        return Message(copy, sends, receives)

    def columns(plane, count):
        return pl.ds(pl.multiple_of(plane * north, north), count * north)

    barrier = pltpu.get_barrier_semaphore()
    for device, exists, _ in ways.values():

        @pl.when(exists)
        def _(device=device):
            pl.semaphore_signal(barrier, inc=1, device_id=device, device_id_type=MESH)

    local = [
        pltpu.make_async_copy(perm_hbm, perm_v, local_sem.at[PERM]),
        pltpu.make_async_copy(mask_hbm, mask_v, local_sem.at[MASK]),
        pltpu.make_async_copy(width_hbm, width_s, local_sem.at[WIDTH]),
        pltpu.make_async_copy(left_hbm, left_v, local_sem.at[LEFT]),
        pltpu.make_async_copy(right_hbm, right_v, local_sem.at[RIGHT]),
        pltpu.make_async_copy(own_hbm, own_v, local_sem.at[OWN]),
    ]
    for index in (PERM, MASK, WIDTH, OWN, LEFT, RIGHT):
        local[index].start()
    low_layer = layers.bit_length() - 1
    pick_row, pick_col = iota((2 * basis, rows), 0), iota((2 * basis, rows), 1)
    wanted = jnp.where(pick_row < basis, pick_row * layers + layers - 1, (pick_row - basis) * layers)
    pick_v[...] = (pick_col == wanted).astype(f32).astype(bf16)
    pair = 2 * north
    r, c = iota((pair, pair), 0), iota((pair, pair), 1)
    plane_bit = north.bit_length() - 1
    one_plane = (r >> plane_bit) == (c >> plane_bit)
    gap = r - c
    shift_v[0] = jnp.where((gap == 1) & one_plane, 1.0, 0.0).astype(bf16)
    beside = (jnp.abs(gap) == 1) & one_plane
    shift_v[1] = jnp.where(beside | (jnp.abs(gap) == north), 1.0, 0.0).astype(bf16)
    r, c = iota((rows, rows), 0), iota((rows, rows), 1)
    gap = r - c
    one_field = (r >> low_layer) == (c >> low_layer)
    shift_v[2] = jnp.where((jnp.abs(gap) == 1) & one_field, 1.0, 0.0).astype(bf16)
    r_layer, c_layer = r & (layers - 1), c & (layers - 1)
    same = r_layer == c_layer
    weight_v[0] = jnp.where(same, 1.0, 0.0)
    weight_v[1] = jnp.where(same, 0.5 * diagonal_weight, jnp.where(c_layer - r_layer == 1, -1.0, 0.0))
    r, c = iota((rows, basis), 0), iota((rows, basis), 1)
    gather_v[...] = jnp.where((r >> low_layer) == c, 1.0, 0.0).astype(bf16)

    for index in (PERM, MASK, WIDTH):
        local[index].wait()

    factor = 0.05 + 0.95 * mask_v[...].astype(f32)
    for cell in range(cells):
        wide = jnp.broadcast_to(factor[:, cell : cell + 1], (layers, north))
        scale_v[cell] = jnp.sqrt(perm_v[cell] * wide).astype(bf16).astype(f32)
    left_width, right_width = width_s[0, 0, 0], width_s[0, 0, 1]
    strip_out[0, 0:margin] = scale_v[cells - margin : cells].astype(bf16)
    strip_out[0, margin] = jnp.full((layers, north), right_width.astype(f32), f32).astype(bf16)
    strip_out[1, 0:margin] = scale_v[0:margin].astype(bf16)
    strip_out[1, margin] = jnp.full((layers, north), left_width.astype(f32), f32).astype(bf16)

    peers = (
        lax.div(lat + lat_n - 1, lat_n) + lax.div(2 * lat_n - 2 - lat, lat_n)
        + lax.div(dep + depth_n - 1, depth_n) + lax.div(2 * depth_n - 2 - dep, depth_n)
    )
    pl.semaphore_wait(barrier, peers)
    strip_r = remote(STRIP_R, strip_out.at[0], strip_in.at[0], "right")
    strip_l = remote(STRIP_L, strip_out.at[1], strip_in.at[1], "left")
    strip_r.start()
    strip_l.start()
    bulk_r, bulk_l, begins = [], [], []
    begin = 0
    for c, size in enumerate(CHUNKS):
        part = pl.ds(begin, size)
        bulk_r.append(remote(BULK_R + c, right_hbm.at[:, part], land_v.at[0, :, part], "right"))
        bulk_l.append(remote(BULK_L + c, left_hbm.at[:, part], land_v.at[1, :, part], "left"))
        bulk_r[c].start()
        bulk_l[c].start()
        if c == 0:
            edge_r = remote(EDGE_R, own_hbm.at[:, pl.ds(cells - 1, 1)], edge_in, "right")
            edge_r.start()
        begins.append(begin)
        begin += size

    first_own = margin + 1
    first_right = first_own + cells + 1
    for plane in (margin, first_right - 1, first_right + margin):
        field_v[:, plane * north : (plane + 1) * north] = jnp.zeros((rows, north), bf16)

    def scaled(values, factors):
        return (values.astype(f32) * factors[None]).reshape(rows, north).astype(bf16)

    def fill(source, factors, first, count, group, side=None, begin=0):
        def step(index, carry):
            base = begin + index * group
            for j in range(group):
                field_v[:, columns(first + base + j, 1)] = scaled(source[:, base + j], factors(base + j))
            planes_v[:, columns(first + base, group)] = nn(
                pick_v[...], field_v[:, columns(first + base, group)]
            ).astype(bf16)
            if side is not None:
                for j in range(0, group, 2):
                    north_v[side, :, columns(base + j, 2)] = nn(
                        field_v[:, columns(first + base + j, 2)], shift_v[0]
                    ).astype(bf16)
            return carry

        lax.fori_loop(0, count // group, step, 0)

    local[OWN].wait()
    own_up, own_down = [], []
    begin = 0
    for part, size in enumerate(OWN_PARTS):
        fill(own_v, lambda plane: scale_v[plane], first_own, size, 8, None, begin)
        source, target = (pl.ds((first + begin) * north, size * north) for first in (first_own, 0))
        own_up.append(remote(OWN_UP + part, planes_v.at[0:basis, source], stack_v.at[basis : 2 * basis, target], "up"))
        own_down.append(
            remote(OWN_DOWN + part, planes_v.at[basis : 2 * basis, source], stack_v.at[0:basis, target], "down")
        )
        own_up[part].start()
        own_down[part].start()
        begin += size

    def operator(step, carry):
        for part in range(0, 8, 2):
            cell = step * 8 + part
            both = field_v[:, columns(first_own + cell, 2)]
            sums = nn(jnp.concatenate([both, shift_v[2]], 1), jnp.concatenate([shift_v[1], both], 0))
            for j, outer in ((0, -1), (1, 2)):
                middle = both[:, j * north : (j + 1) * north].astype(f32)
                beside = field_v[:, columns(first_own + cell + outer, 1)].astype(f32)
                value = diagonal_weight * middle - sums[:, j * north : (j + 1) * north] - beside
                high, low = split(value)
                high_v[:, columns(cell + j, 1)] = high
                low_v[:, columns(cell + j, 1)] = low
        return carry

    lax.fori_loop(0, cells // 8, operator, 0)

    strip_r.wait_recv()
    strip_l.wait_recv()
    at = iota((margin, layers, north), 0).astype(f32)
    none = jnp.zeros((margin, layers, north), f32)
    from_left = strip_in[0].astype(f32)
    from_right = strip_in[1].astype(f32)
    factor_v[0] = jnp.where(at >= margin - left_width.astype(f32), from_left[:margin], none)
    factor_v[1] = jnp.where(at < right_width.astype(f32), from_right[:margin], none)
    factor_v[2] = jnp.where(at < from_left[margin:], scale_v[0:margin], none)
    factor_v[3] = jnp.where(at >= margin - from_right[margin:], scale_v[cells - margin : cells], none)
    local[LEFT].wait()
    local[RIGHT].wait()
    fill(left_v, lambda plane: factor_v[0, plane], 0, margin, 8, 0)
    fill(right_v, lambda plane: factor_v[1, plane], first_right, margin, 8, 1)
    margin_columns = (pl.ds(0, margin * north), pl.ds(first_right * north, margin * north))
    margin_up = remote(MARGIN_UP, planes_v.at[0:basis, margin_columns[0]], mabove_v.at[0], "up")
    margin_down = remote(
        MARGIN_DOWN, planes_v.at[basis : 2 * basis, margin_columns[1]], mabove_v.at[1], "down"
    )
    margin_up.start()
    margin_down.start()

    def gathered(*kept):
        summed = jnp.concatenate([jnp.sum(each.reshape(basis, layers, rows), axis=1) for each in kept], 0)
        high, rest = split_rest(summed)
        middle, rest = split_rest(rest)
        return nn(
            jnp.concatenate([high, middle, rest.astype(bf16)], 1),
            jnp.concatenate([gather_v[...], gather_v[...], gather_v[...]], 0),
        )

    own_fields = field_v[:, first_own * north : (first_own + cells) * north]
    own_sum = nt(own_fields, high_v[...]) + nt(own_fields, low_v[...])
    squares, steps = [], []
    for side, first in ((0, 0), (1, first_right)):
        fields = field_v[:, first * north : (first + margin) * north]
        squares.append(nt(fields, fields))
        steps.append(nt(fields, field_v[:, (first + 1) * north : (first + margin + 1) * north]) + nt(fields, north_v[side]))

    def plane_of(plane):
        return field_v[:, plane * north : (plane + 1) * north]

    border = nt(
        jnp.concatenate([plane_of(margin - 1), plane_of(first_right - 2)], 1),
        jnp.concatenate([plane_of(first_own), plane_of(first_right)], 1),
    )
    own_block = gathered(
        weight_v[1] * (squares[0] + squares[1]) + weight_v[0] * (0.5 * own_sum - (steps[0] + steps[1] + border))
    )
    out_ref[1] = own_block + own_block.T

    starts = (0, cells - margin)
    totals, pairs = [None, None], [None, None]

    def receive(c):
        bulk_r[c].wait_recv()
        bulk_l[c].wait_recv()
        first, size = begins[c], CHUNKS[c]
        part = slice(first * north, (first + size) * north)
        for side in range(2):
            for plane in range(first, first + size):
                other_v[side, :, plane * north : (plane + 1) * north] = scaled(
                    land_v[side, :, plane], factor_v[2 + side, plane]
                )
        for side in range(2):
            other = other_v[side, :, part]
            at_own = slice((starts[side] + first) * north, (starts[side] + first + size) * north)
            term = nt(other, high_v[:, at_own]) + nt(other, low_v[:, at_own])
            totals[side] = term if c == 0 else totals[side] + term
            stack_v[2 * basis : 4 * basis, at_own] = nn(pick_v[...], other).astype(bf16)

    def meet(first, size):
        for side in range(2):
            at_own = slice((starts[side] + first) * north, (starts[side] + first + size) * north)
            stack = stack_v[:, at_own]
            term = nt(stack, stack)
            pairs[side] = term if pairs[side] is None else pairs[side] + term

    receive(0)
    for copy in (*own_up, *own_down):
        copy.wait_recv()
    across = nt(planes_v[:, first_own * north : (first_own + cells) * north], stack_v[0 : 2 * basis])
    for c in range(1, len(CHUNKS) - 1):
        receive(c)
    edge_r.wait_recv()
    edge = scaled(edge_in[:, 0], strip_in[0, margin - 1].astype(f32))
    far = jnp.concatenate([edge, other_v[0, :, 0:north]], 1)
    near = -jnp.concatenate([plane_of(first_own), plane_of(margin - 1)], 1)
    totals[0] = totals[0] + nt(far, near)
    meet(0, begins[-1])
    margin_up.wait_recv()
    margin_down.wait_recv()
    left_bottom = planes_v[basis : 2 * basis, margin_columns[0]]
    right_top = planes_v[0:basis, margin_columns[1]]
    across_down = across[basis:, basis:] + nt(left_bottom, mabove_v[0])
    across_up = across[:basis, :basis] + nt(right_top, mabove_v[1])
    margin_to_down = nt(mabove_v[0], left_bottom)
    margin_to_up = nt(mabove_v[1], right_top)
    receive(len(CHUNKS) - 1)
    meet(begins[-1], CHUNKS[-1])

    with_left, with_right = (both[: 2 * basis, 2 * basis :] for both in pairs)
    blank = jnp.zeros((basis, basis), f32)
    part_out[2] = jnp.concatenate([with_left[:basis, :basis], margin_to_up, with_right[:basis, :basis], blank], 1)
    part_out[3] = jnp.concatenate([with_left[basis:, basis:], margin_to_down, with_right[basis:, basis:], blank], 1)
    fold = iota((basis, 2 * basis), 1) < basis
    turned = [
        jnp.where(fold, both[2 * basis : 3 * basis, : 2 * basis], both[3 * basis :, : 2 * basis]) for both in pairs
    ]
    both_rows = gathered(weight_v[0] * totals[0], weight_v[0] * totals[1])
    rows_of_left, rows_of_right = both_rows[:basis], both_rows[basis:]
    part_out[1] = jnp.concatenate([turned[0], rows_of_left, blank], 1)
    part_out[0] = jnp.concatenate([turned[1], rows_of_right, blank], 1)
    parts = [
        remote(PART_R, part_out.at[0], part_in.at[0], "right"),
        remote(PART_L, part_out.at[1], part_in.at[1], "left"),
        remote(PART_UP, part_out.at[2], part_in.at[2], "up"),
        remote(PART_DOWN, part_out.at[3], part_in.at[3], "down"),
    ]
    for copy in parts:
        copy.start()

    out_ref[0] = rows_of_left.T
    out_ref[2] = rows_of_right.T
    out_ref[4] = across_down
    out_ref[7] = across_up
    for copy in [
        strip_r, strip_l, edge_r, *own_up, *own_down, margin_up, margin_down, *bulk_r, *bulk_l,
    ]:
        copy.wait_send()
    for copy in parts:
        copy.wait_recv()
    west, east, below, above = part_in[0], part_in[1], part_in[2], part_in[3]

    def inside(condition, block):
        return jnp.where(jnp.full(block.shape, condition.astype(jnp.int32), jnp.int32) > 0, block, jnp.zeros_like(block))

    out_ref[0] = inside(has_west, out_ref[0] + west[:, 2 * basis : 3 * basis])
    out_ref[2] = inside(has_east, out_ref[2] + east[:, 2 * basis : 3 * basis])
    out_ref[3] = inside(has_below & has_west, -(below[:, :basis] + west[:, basis : 2 * basis]))
    out_ref[4] = inside(has_below, -(below[:, basis : 2 * basis] + out_ref[4]))
    out_ref[5] = inside(has_below & has_east, -(below[:, 2 * basis : 3 * basis] + east[:, basis : 2 * basis]))
    out_ref[6] = inside(has_above & has_west, -(above[:, :basis] + west[:, :basis]))
    out_ref[7] = inside(has_above, -(above[:, basis : 2 * basis] + out_ref[7]))
    out_ref[8] = inside(has_above & has_east, -(above[:, 2 * basis : 3 * basis] + east[:, :basis]))
    for copy in parts:
        copy.wait_send()


def hand_out(blocks_ref, lateral_ref, vertical_ref, sems):
    copies = [
        pltpu.make_async_copy(blocks_ref.at[0:3], lateral_ref.at[0, 0], sems.at[0]),
        pltpu.make_async_copy(blocks_ref.at[3:6], vertical_ref.at[0, 0, 0], sems.at[1]),
        pltpu.make_async_copy(blocks_ref.at[6:9], vertical_ref.at[0, 0, 1], sems.at[2]),
    ]
    for copy in copies:
        copy.start()
    for copy in copies:
        copy.wait()


def body(lat_n, depth_n, own_basis, left_margin, right_margin, permeability, cluster_mask, intersection_width):
    basis, cells, layers, north = own_basis.shape
    margin = left_margin.shape[1]
    rows = basis * layers
    planes = cells + 2 * margin + 3
    any_space = pl.BlockSpec(memory_space=pl.ANY)
    vmem = pl.BlockSpec(memory_space=pltpu.VMEM)
    scratch = [
        pltpu.VMEM(own_basis.shape, bf16),
        pltpu.VMEM(left_margin.shape, bf16),
        pltpu.VMEM(right_margin.shape, bf16),
        pltpu.VMEM(permeability.shape, f32),
        pltpu.VMEM((layers, cells), jnp.int32),
        pltpu.SMEM(intersection_width.shape, jnp.int32),
        pltpu.VMEM((cells, layers, north), f32),
        pltpu.VMEM((2, margin + 1, layers, north), bf16),
        pltpu.VMEM((2, margin + 1, layers, north), bf16),
        pltpu.VMEM((4, margin, layers, north), f32),
        pltpu.VMEM((2 * basis, rows), bf16),
        pltpu.VMEM((3, rows, rows), bf16),
        pltpu.VMEM((2, rows, rows), f32),
        pltpu.VMEM((rows, basis), bf16),
        pltpu.VMEM((rows, planes * north), bf16),
        pltpu.VMEM((rows, cells * north), bf16),
        pltpu.VMEM((rows, cells * north), bf16),
        pltpu.VMEM((2, rows, margin * north), bf16),
        pltpu.VMEM((basis, 1, layers, north), bf16),
        pltpu.VMEM((2, basis, margin, layers, north), bf16),
        pltpu.VMEM((2, rows, margin * north), bf16),
        pltpu.VMEM((2 * basis, planes * north), bf16),
        pltpu.VMEM((2, basis, margin * north), bf16),
        pltpu.VMEM((4 * basis, cells * north), bf16),
        pltpu.VMEM((4, basis, 4 * basis), f32),
        pltpu.VMEM((4, basis, 4 * basis), f32),
        pltpu.SemaphoreType.DMA((6,)),
        pltpu.SemaphoreType.DMA((REMOTE,)),
        pltpu.SemaphoreType.DMA((REMOTE,)),
    ]
    blocks = pl.pallas_call(
        functools.partial(kernel, lat_n, depth_n),
        out_shape=jax.ShapeDtypeStruct((9, basis, basis), f32),
        in_specs=[any_space] * 6,
        out_specs=vmem,
        scratch_shapes=scratch,
        compiler_params=pltpu.CompilerParams(
            collective_id=0, has_side_effects=True, vmem_limit_bytes=56 * 1024 * 1024
        ),
    )(own_basis, left_margin, right_margin, permeability, cluster_mask.T, intersection_width)
    return pl.pallas_call(
        hand_out,
        out_shape=(
            jax.ShapeDtypeStruct((1, 1, 3, basis, basis), f32),
            jax.ShapeDtypeStruct((1, 1, 2, 3, basis, basis), f32),
        ),
        in_specs=[vmem],
        out_specs=(any_space, any_space),
        scratch_shapes=[pltpu.SemaphoreType.DMA((3,))],
    )(blocks)


def solution(mesh):
    in_specs = (
        P(None, "lat", "depth", None),
        P(None, "lat", "depth", None),
        P(None, "lat", "depth", None),
        P("lat", "depth", None),
        P("lat", "depth"),
        P("lat", "depth", None),
    )
    out_specs = (P("lat", "depth", None, None, None), P("lat", "depth", None, None, None, None))
    return jax.shard_map(
        functools.partial(body, mesh.shape["lat"], mesh.shape["depth"]),
        mesh=mesh, in_specs=in_specs, out_specs=out_specs, check_vma=False,
    )
```

```python
import functools

import jax
import jax.numpy as jnp
from jax import lax
from jax.experimental import pallas as pl
from jax.experimental.pallas import tpu as pltpu
from jax.sharding import PartitionSpec as P

MESH = pl.DeviceIdType.MESH
f32 = jnp.float32
bf16 = jnp.bfloat16
diagonal_weight = 6.1

CHUNKS = (8, 6, 2)

STRIP_R, STRIP_L, EDGE_R, MARGIN_UP, MARGIN_DOWN, PART_R, PART_L, PART_UP, PART_DOWN = range(9)
OWN_PARTS = (16, 24)
OWN_UP = 9
OWN_DOWN = OWN_UP + len(OWN_PARTS)
BULK_R = OWN_DOWN + len(OWN_PARTS)
BULK_L = BULK_R + len(CHUNKS)
REMOTE = BULK_L + len(CHUNKS)

PERM, MASK, WIDTH, LEFT, RIGHT, OWN = range(6)


def nt(left, right):
    return lax.dot_general(left, right, (((1,), (1,)), ((), ())), preferred_element_type=f32)


def nn(left, right):
    return jnp.dot(left, right, preferred_element_type=f32)


def split(value):
    high = value.astype(bf16)
    return high, (value - high.astype(f32)).astype(bf16)


def split_rest(value):
    high = value.astype(bf16)
    return high, value - high.astype(f32)


def iota(shape, dim):
    return lax.broadcasted_iota(jnp.int32, shape, dim)


class Message:
    def __init__(self, copy, sends, receives):
        self.copy, self.sends, self.receives = copy, sends, receives

    def start(self):
        pl.when(self.sends)(self.copy.start)

    def wait_recv(self):
        pl.when(self.receives)(self.copy.wait_recv)

    def wait_send(self):
        pl.when(self.sends)(self.copy.wait_send)


def kernel(
    lat_n, depth_n,
    own_hbm, left_hbm, right_hbm, perm_hbm, mask_hbm, width_hbm,
    out_ref,
    own_v, left_v, right_v, perm_v, mask_v, width_s,
    scale_v, strip_out, strip_in, factor_v,
    pick_v, shift_v, weight_v, gather_v,
    field_v, high_v, low_v, north_v, edge_in,
    land_v, other_v,
    planes_v, mabove_v, stack_v,
    part_out, part_in,
    local_sem, send_sem, recv_sem,
):
    basis, cells, layers, north = own_hbm.shape
    margin = left_hbm.shape[1]
    rows = basis * layers
    lat, dep = lax.axis_index("lat"), lax.axis_index("depth")
    has_west, has_east, has_below, has_above = lat > 0, lat < lat_n - 1, dep > 0, dep < depth_n - 1
    right = (lax.rem(lat + 1, lat_n), dep)
    left = (lax.rem(lat + lat_n - 1, lat_n), dep)
    up = (lat, lax.rem(dep + 1, depth_n))
    down = (lat, lax.rem(dep + depth_n - 1, depth_n))
    ways = {
        "right": (right, has_east, has_west),
        "left": (left, has_west, has_east),
        "up": (up, has_above, has_below),
        "down": (down, has_below, has_above),
    }

    def remote(index, src, dst, way):
        device, sends, receives = ways[way]
        copy = pltpu.make_async_remote_copy(
            src_ref=src, dst_ref=dst, send_sem=send_sem.at[index], recv_sem=recv_sem.at[index],
            device_id=device, device_id_type=MESH,
        )
        return Message(copy, sends, receives)

    def columns(plane, count):
        return pl.ds(pl.multiple_of(plane * north, north), count * north)

    barrier = pltpu.get_barrier_semaphore()
    for device, exists, _ in ways.values():

        @pl.when(exists)
        def _(device=device):
            pl.semaphore_signal(barrier, inc=1, device_id=device, device_id_type=MESH)

    local = [
        pltpu.make_async_copy(perm_hbm, perm_v, local_sem.at[PERM]),
        pltpu.make_async_copy(mask_hbm, mask_v, local_sem.at[MASK]),
        pltpu.make_async_copy(width_hbm, width_s, local_sem.at[WIDTH]),
        pltpu.make_async_copy(left_hbm, left_v, local_sem.at[LEFT]),
        pltpu.make_async_copy(right_hbm, right_v, local_sem.at[RIGHT]),
        pltpu.make_async_copy(own_hbm, own_v, local_sem.at[OWN]),
    ]
    for index in (PERM, MASK, WIDTH, OWN, LEFT, RIGHT):
        local[index].start()
    low_layer = layers.bit_length() - 1
    pick_row, pick_col = iota((2 * basis, rows), 0), iota((2 * basis, rows), 1)
    wanted = jnp.where(pick_row < basis, pick_row * layers + layers - 1, (pick_row - basis) * layers)
    pick_v[...] = (pick_col == wanted).astype(f32).astype(bf16)
    pair = 2 * north
    r, c = iota((pair, pair), 0), iota((pair, pair), 1)
    plane_bit = north.bit_length() - 1
    one_plane = (r >> plane_bit) == (c >> plane_bit)
    gap = r - c
    shift_v[0] = jnp.where((gap == 1) & one_plane, 1.0, 0.0).astype(bf16)
    beside = (jnp.abs(gap) == 1) & one_plane
    shift_v[1] = jnp.where(beside | (jnp.abs(gap) == north), 1.0, 0.0).astype(bf16)
    r, c = iota((rows, rows), 0), iota((rows, rows), 1)
    gap = r - c
    one_field = (r >> low_layer) == (c >> low_layer)
    shift_v[2] = jnp.where((jnp.abs(gap) == 1) & one_field, 1.0, 0.0).astype(bf16)
    r_layer, c_layer = r & (layers - 1), c & (layers - 1)
    same = r_layer == c_layer
    weight_v[0] = jnp.where(same, 1.0, 0.0)
    weight_v[1] = jnp.where(same, 0.5 * diagonal_weight, jnp.where(c_layer - r_layer == 1, -1.0, 0.0))
    r, c = iota((rows, basis), 0), iota((rows, basis), 1)
    gather_v[...] = jnp.where((r >> low_layer) == c, 1.0, 0.0).astype(bf16)

    for index in (PERM, MASK, WIDTH):
        local[index].wait()

    factor = 0.05 + 0.95 * mask_v[...].astype(f32)
    for cell in range(cells):
        wide = jnp.broadcast_to(factor[:, cell : cell + 1], (layers, north))
        scale_v[cell] = jnp.sqrt(perm_v[cell] * wide).astype(bf16).astype(f32)
    left_width, right_width = width_s[0, 0, 0], width_s[0, 0, 1]
    strip_out[0, 0:margin] = scale_v[cells - margin : cells].astype(bf16)
    strip_out[0, margin] = jnp.full((layers, north), right_width.astype(f32), f32).astype(bf16)
    strip_out[1, 0:margin] = scale_v[0:margin].astype(bf16)
    strip_out[1, margin] = jnp.full((layers, north), left_width.astype(f32), f32).astype(bf16)

    peers = (
        lax.div(lat + lat_n - 1, lat_n) + lax.div(2 * lat_n - 2 - lat, lat_n)
        + lax.div(dep + depth_n - 1, depth_n) + lax.div(2 * depth_n - 2 - dep, depth_n)
    )
    pl.semaphore_wait(barrier, peers)
    strip_r = remote(STRIP_R, strip_out.at[0], strip_in.at[0], "right")
    strip_l = remote(STRIP_L, strip_out.at[1], strip_in.at[1], "left")
    strip_r.start()
    strip_l.start()
    bulk_r, bulk_l, begins = [], [], []
    begin = 0
    for c, size in enumerate(CHUNKS):
        part = pl.ds(begin, size)
        bulk_r.append(remote(BULK_R + c, right_hbm.at[:, part], land_v.at[0, :, part], "right"))
        bulk_l.append(remote(BULK_L + c, left_hbm.at[:, part], land_v.at[1, :, part], "left"))
        bulk_r[c].start()
        bulk_l[c].start()
        if c == 1:
            edge_r = remote(EDGE_R, own_hbm.at[:, pl.ds(cells - 1, 1)], edge_in, "right")
            edge_r.start()
        begins.append(begin)
        begin += size

    first_own = margin + 1
    first_right = first_own + cells + 1
    for plane in (margin, first_right - 1, first_right + margin):
        field_v[:, plane * north : (plane + 1) * north] = jnp.zeros((rows, north), bf16)

    def scaled(values, factors):
        return (values.astype(f32) * factors[None]).reshape(rows, north).astype(bf16)

    def fill(source, factors, first, count, group, side=None, begin=0):
        def step(index, carry):
            base = begin + index * group
            for j in range(group):
                field_v[:, columns(first + base + j, 1)] = scaled(source[:, base + j], factors(base + j))
            planes_v[:, columns(first + base, group)] = nn(
                pick_v[...], field_v[:, columns(first + base, group)]
            ).astype(bf16)
            if side is not None:
                for j in range(0, group, 2):
                    north_v[side, :, columns(base + j, 2)] = nn(
                        field_v[:, columns(first + base + j, 2)], shift_v[0]
                    ).astype(bf16)
            return carry

        lax.fori_loop(0, count // group, step, 0)

    local[OWN].wait()
    own_up, own_down = [], []
    begin = 0
    for part, size in enumerate(OWN_PARTS):
        fill(own_v, lambda plane: scale_v[plane], first_own, size, 8, None, begin)
        source, target = (pl.ds((first + begin) * north, size * north) for first in (first_own, 0))
        own_up.append(remote(OWN_UP + part, planes_v.at[0:basis, source], stack_v.at[basis : 2 * basis, target], "up"))
        own_down.append(
            remote(OWN_DOWN + part, planes_v.at[basis : 2 * basis, source], stack_v.at[0:basis, target], "down")
        )
        own_up[part].start()
        own_down[part].start()
        begin += size

    def operator(step, carry):
        for part in range(0, 8, 2):
            cell = step * 8 + part
            both = field_v[:, columns(first_own + cell, 2)]
            sums = nn(jnp.concatenate([both, shift_v[2]], 1), jnp.concatenate([shift_v[1], both], 0))
            for j, outer in ((0, -1), (1, 2)):
                middle = both[:, j * north : (j + 1) * north].astype(f32)
                beside = field_v[:, columns(first_own + cell + outer, 1)].astype(f32)
                value = diagonal_weight * middle - sums[:, j * north : (j + 1) * north] - beside
                high, low = split(value)
                high_v[:, columns(cell + j, 1)] = high
                low_v[:, columns(cell + j, 1)] = low
        return carry

    lax.fori_loop(0, cells // 8, operator, 0)

    strip_r.wait_recv()
    strip_l.wait_recv()
    at = iota((margin, layers, north), 0).astype(f32)
    none = jnp.zeros((margin, layers, north), f32)
    from_left = strip_in[0].astype(f32)
    from_right = strip_in[1].astype(f32)
    factor_v[0] = jnp.where(at >= margin - left_width.astype(f32), from_left[:margin], none)
    factor_v[1] = jnp.where(at < right_width.astype(f32), from_right[:margin], none)
    factor_v[2] = jnp.where(at < from_left[margin:], scale_v[0:margin], none)
    factor_v[3] = jnp.where(at >= margin - from_right[margin:], scale_v[cells - margin : cells], none)
    local[LEFT].wait()
    local[RIGHT].wait()
    fill(left_v, lambda plane: factor_v[0, plane], 0, margin, 8, 0)
    fill(right_v, lambda plane: factor_v[1, plane], first_right, margin, 8, 1)
    margin_columns = (pl.ds(0, margin * north), pl.ds(first_right * north, margin * north))
    margin_up = remote(MARGIN_UP, planes_v.at[0:basis, margin_columns[0]], mabove_v.at[0], "up")
    margin_down = remote(
        MARGIN_DOWN, planes_v.at[basis : 2 * basis, margin_columns[1]], mabove_v.at[1], "down"
    )
    margin_up.start()
    margin_down.start()

    def gathered(*kept):
        summed = jnp.concatenate([jnp.sum(each.reshape(basis, layers, rows), axis=1) for each in kept], 0)
        high, rest = split_rest(summed)
        middle, rest = split_rest(rest)
        return nn(
            jnp.concatenate([high, middle, rest.astype(bf16)], 1),
            jnp.concatenate([gather_v[...], gather_v[...], gather_v[...]], 0),
        )

    own_fields = field_v[:, first_own * north : (first_own + cells) * north]
    own_sum = nt(own_fields, high_v[...]) + nt(own_fields, low_v[...])
    squares, steps = [], []
    for side, first in ((0, 0), (1, first_right)):
        fields = field_v[:, first * north : (first + margin) * north]
        squares.append(nt(fields, fields))
        steps.append(nt(fields, field_v[:, (first + 1) * north : (first + margin + 1) * north]) + nt(fields, north_v[side]))

    def plane_of(plane):
        return field_v[:, plane * north : (plane + 1) * north]

    border = nt(
        jnp.concatenate([plane_of(margin - 1), plane_of(first_right - 2)], 1),
        jnp.concatenate([plane_of(first_own), plane_of(first_right)], 1),
    )
    own_block = gathered(
        weight_v[1] * (squares[0] + squares[1]) + weight_v[0] * (0.5 * own_sum - (steps[0] + steps[1] + border))
    )
    out_ref[1] = own_block + own_block.T

    starts = (0, cells - margin)
    totals, pairs = [None, None], [None, None]

    def receive(c):
        bulk_r[c].wait_recv()
        bulk_l[c].wait_recv()
        first, size = begins[c], CHUNKS[c]
        part = slice(first * north, (first + size) * north)
        for side in range(2):
            for plane in range(first, first + size):
                other_v[side, :, plane * north : (plane + 1) * north] = scaled(
                    land_v[side, :, plane], factor_v[2 + side, plane]
                )
        for side in range(2):
            other = other_v[side, :, part]
            at_own = slice((starts[side] + first) * north, (starts[side] + first + size) * north)
            term = nt(other, high_v[:, at_own]) + nt(other, low_v[:, at_own])
            totals[side] = term if c == 0 else totals[side] + term
            stack_v[2 * basis : 4 * basis, at_own] = nn(pick_v[...], other).astype(bf16)

    def meet(first, size):
        for side in range(2):
            at_own = slice((starts[side] + first) * north, (starts[side] + first + size) * north)
            stack = stack_v[:, at_own]
            term = nt(stack, stack)
            pairs[side] = term if pairs[side] is None else pairs[side] + term

    receive(0)
    for copy in (*own_up, *own_down):
        copy.wait_recv()
    across = nt(planes_v[:, first_own * north : (first_own + cells) * north], stack_v[0 : 2 * basis])
    for c in range(1, len(CHUNKS) - 1):
        receive(c)
    edge_r.wait_recv()
    edge = scaled(edge_in[:, 0], strip_in[0, margin - 1].astype(f32))
    far = jnp.concatenate([edge, other_v[0, :, 0:north]], 1)
    near = -jnp.concatenate([plane_of(first_own), plane_of(margin - 1)], 1)
    totals[0] = totals[0] + nt(far, near)
    meet(0, begins[-1])
    margin_up.wait_recv()
    margin_down.wait_recv()
    left_bottom = planes_v[basis : 2 * basis, margin_columns[0]]
    right_top = planes_v[0:basis, margin_columns[1]]
    across_down = across[basis:, basis:] + nt(left_bottom, mabove_v[0])
    across_up = across[:basis, :basis] + nt(right_top, mabove_v[1])
    margin_to_down = nt(mabove_v[0], left_bottom)
    margin_to_up = nt(mabove_v[1], right_top)
    receive(len(CHUNKS) - 1)
    meet(begins[-1], CHUNKS[-1])

    with_left, with_right = (both[: 2 * basis, 2 * basis :] for both in pairs)
    blank = jnp.zeros((basis, basis), f32)
    part_out[2] = jnp.concatenate([with_left[:basis, :basis], margin_to_up, with_right[:basis, :basis], blank], 1)
    part_out[3] = jnp.concatenate([with_left[basis:, basis:], margin_to_down, with_right[basis:, basis:], blank], 1)
    fold = iota((basis, 2 * basis), 1) < basis
    turned = [
        jnp.where(fold, both[2 * basis : 3 * basis, : 2 * basis], both[3 * basis :, : 2 * basis]) for both in pairs
    ]
    both_rows = gathered(weight_v[0] * totals[0], weight_v[0] * totals[1])
    rows_of_left, rows_of_right = both_rows[:basis], both_rows[basis:]
    part_out[1] = jnp.concatenate([turned[0], rows_of_left, blank], 1)
    part_out[0] = jnp.concatenate([turned[1], rows_of_right, blank], 1)
    parts = [
        remote(PART_R, part_out.at[0], part_in.at[0], "right"),
        remote(PART_L, part_out.at[1], part_in.at[1], "left"),
        remote(PART_UP, part_out.at[2], part_in.at[2], "up"),
        remote(PART_DOWN, part_out.at[3], part_in.at[3], "down"),
    ]
    for copy in parts:
        copy.start()

    out_ref[0] = rows_of_left.T
    out_ref[2] = rows_of_right.T
    out_ref[4] = across_down
    out_ref[7] = across_up
    for copy in [
        strip_r, strip_l, edge_r, *own_up, *own_down, margin_up, margin_down, *bulk_r, *bulk_l,
    ]:
        copy.wait_send()
    for copy in parts:
        copy.wait_recv()
    west, east, below, above = part_in[0], part_in[1], part_in[2], part_in[3]

    def inside(condition, block):
        return jnp.where(jnp.full(block.shape, condition.astype(jnp.int32), jnp.int32) > 0, block, jnp.zeros_like(block))

    out_ref[0] = inside(has_west, out_ref[0] + west[:, 2 * basis : 3 * basis])
    out_ref[2] = inside(has_east, out_ref[2] + east[:, 2 * basis : 3 * basis])
    out_ref[3] = inside(has_below & has_west, -(below[:, :basis] + west[:, basis : 2 * basis]))
    out_ref[4] = inside(has_below, -(below[:, basis : 2 * basis] + out_ref[4]))
    out_ref[5] = inside(has_below & has_east, -(below[:, 2 * basis : 3 * basis] + east[:, basis : 2 * basis]))
    out_ref[6] = inside(has_above & has_west, -(above[:, :basis] + west[:, :basis]))
    out_ref[7] = inside(has_above, -(above[:, basis : 2 * basis] + out_ref[7]))
    out_ref[8] = inside(has_above & has_east, -(above[:, 2 * basis : 3 * basis] + east[:, :basis]))
    for copy in parts:
        copy.wait_send()


def hand_out(blocks_ref, lateral_ref, vertical_ref, sems):
    copies = [
        pltpu.make_async_copy(blocks_ref.at[0:3], lateral_ref.at[0, 0], sems.at[0]),
        pltpu.make_async_copy(blocks_ref.at[3:6], vertical_ref.at[0, 0, 0], sems.at[1]),
        pltpu.make_async_copy(blocks_ref.at[6:9], vertical_ref.at[0, 0, 1], sems.at[2]),
    ]
    for copy in copies:
        copy.start()
    for copy in copies:
        copy.wait()


def body(lat_n, depth_n, own_basis, left_margin, right_margin, permeability, cluster_mask, intersection_width):
    basis, cells, layers, north = own_basis.shape
    margin = left_margin.shape[1]
    rows = basis * layers
    planes = cells + 2 * margin + 3
    any_space = pl.BlockSpec(memory_space=pl.ANY)
    vmem = pl.BlockSpec(memory_space=pltpu.VMEM)
    scratch = [
        pltpu.VMEM(own_basis.shape, bf16),
        pltpu.VMEM(left_margin.shape, bf16),
        pltpu.VMEM(right_margin.shape, bf16),
        pltpu.VMEM(permeability.shape, f32),
        pltpu.VMEM((layers, cells), jnp.int32),
        pltpu.SMEM(intersection_width.shape, jnp.int32),
        pltpu.VMEM((cells, layers, north), f32),
        pltpu.VMEM((2, margin + 1, layers, north), bf16),
        pltpu.VMEM((2, margin + 1, layers, north), bf16),
        pltpu.VMEM((4, margin, layers, north), f32),
        pltpu.VMEM((2 * basis, rows), bf16),
        pltpu.VMEM((3, rows, rows), bf16),
        pltpu.VMEM((2, rows, rows), f32),
        pltpu.VMEM((rows, basis), bf16),
        pltpu.VMEM((rows, planes * north), bf16),
        pltpu.VMEM((rows, cells * north), bf16),
        pltpu.VMEM((rows, cells * north), bf16),
        pltpu.VMEM((2, rows, margin * north), bf16),
        pltpu.VMEM((basis, 1, layers, north), bf16),
        pltpu.VMEM((2, basis, margin, layers, north), bf16),
        pltpu.VMEM((2, rows, margin * north), bf16),
        pltpu.VMEM((2 * basis, planes * north), bf16),
        pltpu.VMEM((2, basis, margin * north), bf16),
        pltpu.VMEM((4 * basis, cells * north), bf16),
        pltpu.VMEM((4, basis, 4 * basis), f32),
        pltpu.VMEM((4, basis, 4 * basis), f32),
        pltpu.SemaphoreType.DMA((6,)),
        pltpu.SemaphoreType.DMA((REMOTE,)),
        pltpu.SemaphoreType.DMA((REMOTE,)),
    ]
    blocks = pl.pallas_call(
        functools.partial(kernel, lat_n, depth_n),
        out_shape=pltpu.VMEM((9, basis, basis), f32),
        in_specs=[any_space] * 6,
        out_specs=vmem,
        scratch_shapes=scratch,
        compiler_params=pltpu.CompilerParams(
            collective_id=0, has_side_effects=True, vmem_limit_bytes=56 * 1024 * 1024
        ),
    )(own_basis, left_margin, right_margin, permeability, cluster_mask.T, intersection_width)
    return pl.pallas_call(
        hand_out,
        out_shape=(
            jax.ShapeDtypeStruct((1, 1, 3, basis, basis), f32),
            jax.ShapeDtypeStruct((1, 1, 2, 3, basis, basis), f32),
        ),
        in_specs=[vmem],
        out_specs=(any_space, any_space),
        scratch_shapes=[pltpu.SemaphoreType.DMA((3,))],
    )(blocks)


def solution(mesh):
    in_specs = (
        P(None, "lat", "depth", None),
        P(None, "lat", "depth", None),
        P(None, "lat", "depth", None),
        P("lat", "depth", None),
        P("lat", "depth"),
        P("lat", "depth", None),
    )
    out_specs = (P("lat", "depth", None, None, None), P("lat", "depth", None, None, None, None))
    return jax.shard_map(
        functools.partial(body, mesh.shape["lat"], mesh.shape["depth"]),
        mesh=mesh, in_specs=in_specs, out_specs=out_specs, check_vma=False,
    )
```
